32 devices in a mesh: seq: 8 (over y, x, core), grp: 4 (over z).
Axes of the slice: x: 2, y: 2, z: 4, core: 2. Of those that a mesh axis runs over, the one named last changes fastest.
Arguments:
- tokens: bfloat16 [8192, 2048], P(('seq', 'grp')), may hold values from -6 to 6
- first_gain: bfloat16 [2048], P('seq'), may hold values from 0.5 to 1.5
- first_bias: bfloat16 [2048], P('seq'), may hold values from -1 to 1
- query_weight: bfloat16 [2048, 2048], P('seq', 'grp'), may hold values from -0.125 to 0.125
- key_weight: bfloat16 [2048, 2048], P('seq', 'grp'), may hold values from -0.125 to 0.125
- value_weight: bfloat16 [2048, 4096], P('seq', 'grp'), may hold values from -0.125 to 0.125
- gate_weight: bfloat16 [2048, 4096], P('seq', 'grp'), may hold values from -0.125 to 0.125
- group_gain: bfloat16 [512, 8], P('seq', 'grp'), may hold values from 0.5 to 1.5
- group_bias: bfloat16 [512, 8], P('seq', 'grp'), may hold values from -1 to 1
- out_weight: bfloat16 [4096, 2048], P('seq'), may hold values from -0.1875 to 0.1875
- second_gain: bfloat16 [2048], P('seq'), may hold values from 0.5 to 1.5
- second_bias: bfloat16 [2048], P('seq'), may hold values from -1 to 1
- up_weight: bfloat16 [2048, 4096], P('seq'), may hold values from -0.125 to 0.125
- up_bias: bfloat16 [4096], P('seq'), may hold values from -1 to 1
- down_weight: bfloat16 [4096, 2048], P('seq'), may hold values from -0.125 to 0.125
- down_bias: bfloat16 [2048], P('seq'), may hold values from -1 to 1
- cotangent: bfloat16 [8192, 2048], P(('seq', 'grp')), may hold values from -6 to 6
- doc_lengths: int32 [3], replicated, may hold values from 1024 to 4096, as said below
- windows: int32 [4], P('grp'), may hold values from 512 to 1024
Outputs:
- mixed: bfloat16 [8192, 2048], P(('seq', 'grp'))
- tokens_grad: bfloat16 [8192, 2048], P(('seq', 'grp'))
- first_gain_grad: float32 [2048], P('seq')
- first_bias_grad: float32 [2048], P('seq')
- query_grad: float32 [2048, 2048], P('seq', 'grp')
- key_grad: float32 [2048, 2048], P('seq', 'grp')
- value_grad: float32 [2048, 4096], P('seq', 'grp')
- gate_grad: float32 [2048, 4096], P('seq', 'grp')
- group_gain_grad: float32 [512, 8], P('seq', 'grp')
- group_bias_grad: float32 [512, 8], P('seq', 'grp')
- out_grad: float32 [4096, 2048], P('seq')
- second_gain_grad: float32 [2048], P('seq')
- second_bias_grad: float32 [2048], P('seq')
- up_grad: float32 [2048, 4096], P('seq')
- up_bias_grad: float32 [4096], P('seq')
- down_grad: float32 [4096, 2048], P('seq')
- down_bias_grad: float32 [2048], P('seq')
The draws below stay inside these ranges and needn't reach their ends.
Inputs may be any that keep to these rules, and one draw needn't show every extreme that they name: `doc_lengths`: the 3 documents fill the 8192 tokens in order; each is 1024 tokens or more and exactly one is 4096 long.
All inputs are finite; a program needn't handle non-finite values.
Results may differ from the reference program's by a relative error of at most 0.023.
Values may be sent and summed in bfloat16 or wider, within the bound.
No kernel may reach another device: no remote copies, remote signals or barrier semaphores. Data moves between devices by JAX's collectives and lax.ppermute only.
A program may use at most 384 MiB of HBM per device.

```python
import jax
import jax.numpy as jnp
from jax import lax

D = 2048
HEADS = 8
KD = 256
VD = 512
FF = 4096
TOK_DEV = 256
STRETCH = 512
GROUPS = 4
RET_DEV = 1024
TOKENS = 8192
DOCS = 3
MIN_DOC = 1024
LONG_DOC = 4096
N_GRP = 4


def draw_doc_lengths(key, part):
    key = jax.random.fold_in(key, 11)
    first, second = jax.random.split(key)
    extra_total = TOKENS - LONG_DOC - (DOCS - 1) * MIN_DOC
    heavy = jnp.left_shift(jnp.int32(1), jax.random.randint(first, (DOCS - 1,), 0, 7))
    share = extra_total * heavy // jnp.sum(heavy)
    share = share.at[DOCS - 2].add(extra_total - jnp.sum(share))
    others = MIN_DOC + share
    lengths = jnp.concatenate([jnp.full((1,), LONG_DOC, jnp.int32), others.astype(jnp.int32)])
    order = jax.random.permutation(second, DOCS)
    return lengths[order].astype(jnp.int32)


def place_ends(values, rng, low, high):
    longest = values.shape.index(max(values.shape))
    spots = []
    for shift in (0, 1):
        where = [jax.random.randint(jax.random.fold_in(rng, axis), (), 0, length) for axis, length in enumerate(values.shape)]
        where[longest] = (where[longest] + shift) % values.shape[longest]
        spots.append(tuple(where))
    return values.at[spots[0]].set(low).at[spots[1]].set(high)


def block_levels(key, dims, cuts, low, high):
    level = 1.0
    for position, parts in cuts:
        heights = jax.random.uniform(jax.random.fold_in(jax.random.fold_in(key, 6), position), (parts,), jnp.float32, low / len(cuts), high / len(cuts))
        level = level * jnp.repeat(jnp.exp(heights), dims[position] // parts).reshape((-1,) + (1,) * (len(dims) - 1 - position))
    return level


def bell_draw(own_key, shape, scale, bound, cuts=(), kind=jnp.bfloat16):
    entries = scale * jax.random.normal(own_key, shape, jnp.float32)
    if cuts:
        entries = entries * block_levels(own_key, shape, cuts, -0.22, 0.18)
    return jnp.clip(entries, -bound, bound).astype(kind)


def setup_inputs(seed: int = 0) -> dict:
    splits = jax.random.split(jax.random.key(seed), 20)
    return {
        "tokens": bell_draw(splits[0], (TOKENS, D), 1.0, 6.0, ((0, 32),)),
        "first_gain": jnp.clip(1.0 + 0.1 * jax.random.normal(splits[1], (D,), jnp.float32), 0.5, 1.5).astype(jnp.bfloat16),
        "first_bias": bell_draw(splits[2], (D,), 0.2, 1.0, ((0, 8),)),
        "query_weight": bell_draw(splits[3], (D, HEADS * KD), D ** -0.5, 0.125, ((0, 8), (1, 4))),
        "key_weight": bell_draw(splits[4], (D, HEADS * KD), D ** -0.5, 0.125, ((0, 8), (1, 4))),
        "value_weight": bell_draw(splits[5], (D, HEADS * VD), D ** -0.5, 0.125, ((0, 8), (1, 4))),
        "gate_weight": bell_draw(splits[6], (D, HEADS * VD), D ** -0.5, 0.125, ((0, 8), (1, 4))),
        "group_gain": jnp.clip(1.0 + 0.1 * jax.random.normal(splits[7], (VD, HEADS), jnp.float32), 0.5, 1.5).astype(jnp.bfloat16),
        "group_bias": bell_draw(splits[8], (VD, HEADS), 0.2, 1.0, ((0, 8), (1, 4))),
        "out_weight": bell_draw(splits[9], (HEADS * VD, D), (HEADS * VD // 4) ** -0.5, 0.1875, ((0, 8),)),
        "second_gain": jnp.clip(1.0 + 0.1 * jax.random.normal(splits[10], (D,), jnp.float32), 0.5, 1.5).astype(jnp.bfloat16),
        "second_bias": bell_draw(splits[11], (D,), 0.2, 1.0, ((0, 8),)),
        "up_weight": bell_draw(splits[12], (D, FF), D ** -0.5, 0.125, ((0, 8),)),
        "up_bias": bell_draw(splits[13], (FF,), 0.2, 1.0, ((0, 8),)),
        "down_weight": bell_draw(splits[14], (FF, D), (FF // 2) ** -0.5, 0.125, ((0, 8),)),
        "down_bias": bell_draw(splits[15], (D,), 0.2, 1.0, ((0, 8),)),
        "cotangent": bell_draw(splits[16], (TOKENS, D), 1.0, 6.0, ((0, 32),)),
        "doc_lengths": draw_doc_lengths(jax.random.fold_in(splits[19], 71), 0),
        "windows": place_ends(jax.random.randint(splits[18], (GROUPS,), TOK_DEV * N_GRP // 2, TOK_DEV * N_GRP + 1), jax.random.fold_in(splits[18], 1), TOK_DEV * N_GRP // 2, TOK_DEV * N_GRP).astype(jnp.int32),
    }


EPSILON = 1e-05

@jax.custom_vjp
def low(v):
    return lax.optimization_barrier(v.astype(jnp.bfloat16)).astype(jnp.float32)

@jax.custom_vjp
def low_back(v):
    return v

def low_keep(v):
    return (low(v), None)

def low_pass(kept, grad):
    return (grad,)

def back_keep(v):
    return (v, None)

def back_low(kept, grad):
    return (low(grad),)
low.defvjp(low_keep, low_pass)
low_back.defvjp(back_keep, back_low)

def layer_norm(values, gain, bias):
    center = values - lax.optimization_barrier(jnp.mean(values, axis=-1, keepdims=True))
    spread = lax.optimization_barrier(jnp.mean(center * center, axis=-1, keepdims=True))
    return center * lax.rsqrt(spread + EPSILON) * gain + bias

def document_table(doc_lengths, positions):
    ends = jnp.cumsum(doc_lengths, dtype=jnp.int32)
    after = (positions[:, None] >= ends[None, :]).astype(jnp.int32)
    documents = lax.optimization_barrier(jnp.sum(after, axis=1, dtype=jnp.int32))
    starts = lax.optimization_barrier(jnp.sum(after * doc_lengths[None, :], axis=1, dtype=jnp.int32))
    return (documents, positions - starts)

def rotary_table(places, width):
    half = width // 2
    freqs = 10000.0 ** (-jnp.arange(half, dtype=jnp.float32) / (half - 1))
    angles = places.astype(jnp.float32)[:, None] * freqs[None, :]
    cosine = jnp.cos(angles)
    sine = jnp.sin(angles)
    return (jnp.concatenate([cosine, cosine], axis=1), jnp.concatenate([sine, sine], axis=1))

def rotate(values, cosine, sine):
    half = values.shape[-1] // 2
    turned = jnp.concatenate([-values[..., half:], values[..., :half]], axis=-1)
    return values * cosine[:, None, :] + turned * sine[:, None, :]

def decay_mask(query_pos, key_pos, query_doc, key_doc, log_decay, window):
    distance = query_pos[:, None] - key_pos[None, :]
    inside = (distance >= 0) & (query_doc[:, None] == key_doc[None, :]) & (key_pos[None, :] >= 0)
    inside = inside[None] & (distance[None] < window[:, None, None])
    steps = jnp.where(inside, distance[None], 0).astype(jnp.float32)
    return jnp.where(inside, jnp.exp(steps * log_decay[:, None, None]), 0.0)

def gate_norm(retained, gate_pre, gain, bias):
    center = retained - lax.optimization_barrier(jnp.mean(retained, axis=-1, keepdims=True))
    spread = lax.optimization_barrier(jnp.mean(center * center, axis=-1, keepdims=True))
    grouped = center * lax.rsqrt(spread + EPSILON) * gain.T[None] + bias.T[None]
    return jax.nn.silu(gate_pre) * grouped.reshape(retained.shape[0], -1)

def forward(params, doc_lengths, windows):
    inputs, gain_one, bias_one, query_weight, key_weight, value_weight, gate_weight, group_gain, group_bias, out_weight, gain_two, bias_two, up_weight, up_bias, down_weight, down_bias = params
    highest = lax.Precision.HIGHEST
    positions = jnp.arange(TOKENS, dtype=jnp.int32)
    documents, places = document_table(doc_lengths, positions)
    cosine, sine = rotary_table(places, KD)
    normed = low(layer_norm(inputs, gain_one, bias_one))
    query_pre = low_back(jnp.dot(normed, query_weight, precision=highest))
    key_pre = low_back(jnp.dot(normed, key_weight, precision=highest))
    values = low(low_back(jnp.dot(normed, value_weight, precision=highest))).reshape(TOKENS, HEADS, VD)
    gate_pre = low_back(jnp.dot(normed, gate_weight, precision=highest))
    queries = low(rotate(query_pre.reshape(TOKENS, HEADS, KD), cosine, sine))
    keys = low(rotate(key_pre.reshape(TOKENS, HEADS, KD), cosine, sine) * KD ** (-0.5))
    span = RET_DEV + STRETCH
    key_pad = jnp.concatenate([jnp.zeros((RET_DEV, HEADS, KD), keys.dtype), keys], axis=0)
    value_pad = jnp.concatenate([jnp.zeros((RET_DEV, HEADS, VD), values.dtype), values], axis=0)
    window = jnp.repeat(windows, HEADS // GROUPS)
    log_decay = jnp.log1p(-jnp.exp2(-5.0 - jnp.arange(HEADS, dtype=jnp.float32)))

    def block(index):
        start = index * STRETCH
        query_pos = start + jnp.arange(STRETCH, dtype=jnp.int32)
        key_pos = start - RET_DEV + jnp.arange(span, dtype=jnp.int32)
        query_doc = document_table(doc_lengths, query_pos)[0]
        key_doc = document_table(doc_lengths, key_pos)[0]
        mask = decay_mask(query_pos, key_pos, query_doc, key_doc, log_decay, window)
        block_queries = lax.dynamic_slice_in_dim(queries, start, STRETCH, 0)
        block_keys = lax.dynamic_slice_in_dim(key_pad, start, span, 0)
        block_values = lax.dynamic_slice_in_dim(value_pad, start, span, 0)
        scores = low_back(jnp.einsum('qhd,khd->hqk', block_queries, block_keys, precision=highest))
        weights = low(scores * mask)
        return jnp.einsum('hqk,khe->qhe', weights, block_values, precision=highest)
    blocks = lax.map(jax.checkpoint(block), jnp.arange(TOKENS // STRETCH, dtype=jnp.int32))
    retained = low_back(blocks.reshape(TOKENS, HEADS, VD))
    heads_out = low(low_back(gate_norm(retained, gate_pre, group_gain, group_bias)))
    hidden = inputs + low_back(jnp.dot(heads_out, out_weight, precision=highest))
    normed_two = low(layer_norm(hidden, gain_two, bias_two))
    pre_act = low_back(jnp.dot(normed_two, up_weight, precision=highest) + up_bias)
    activated = low(jax.nn.gelu(pre_act, approximate=False))
    return hidden + jnp.dot(activated, down_weight, precision=highest) + down_bias

def reference(tokens, first_gain, first_bias, query_weight, key_weight, value_weight, gate_weight, group_gain, group_bias, out_weight, second_gain, second_bias, up_weight, up_bias, down_weight, down_bias, cotangent, doc_lengths, windows):
    params = tuple((item.astype(jnp.float32) for item in (tokens, first_gain, first_bias, query_weight, key_weight, value_weight, gate_weight, group_gain, group_bias, out_weight, second_gain, second_bias, up_weight, up_bias, down_weight, down_bias)))
    result, pullback = jax.vjp(lambda *items: forward(items, doc_lengths, windows), *params)
    grads = pullback(cotangent.astype(jnp.float32))
    return (result.astype(jnp.bfloat16), grads[0].astype(jnp.bfloat16), grads[1], grads[2], grads[3], grads[4], grads[5], grads[6], grads[7], grads[8], grads[9], grads[10], grads[11], grads[12], grads[13], grads[14], grads[15])
```

```python
from functools import partial

import jax
import jax.numpy as jnp
from jax import lax
from jax.sharding import PartitionSpec as P

KD = 256
VD = 512
STRETCH = 512
EPSILON = 1e-05

F32 = jnp.float32
BF16 = jnp.bfloat16


def dot(a, b, dims=((1,), (0,))):
    return lax.dot_general(a, b, (dims, ((), ())), preferred_element_type=F32)


def flip(block, bit):
    devices = lax.axis_size("seq")
    return lax.ppermute(block, "seq", [(i, i ^ bit) for i in range(devices)])


def hop(block, by):
    devices = lax.axis_size("seq")
    return lax.ppermute(block, "seq", [(i, i + by) for i in range(devices) if 0 <= i + by < devices])


def turn(block, by):
    groups = lax.axis_size("grp")
    return lax.ppermute(block, "grp", [(i, (i + by) % groups) for i in range(groups)])


def pick(array, index, axis=0):
    return lax.dynamic_index_in_dim(array, index, axis, keepdims=False)


def cut(array, index, size, axis):
    return lax.dynamic_slice_in_dim(array, index * size, size, axis)


def put(array, block, index, axis):
    return lax.dynamic_update_slice_in_dim(array, block, index * block.shape[axis], axis)


def after(block, *others):
    return lax.optimization_barrier((block, *others))[0]


class Stages:
    def __init__(self):
        self.last = ()

    def run(self, *sends, late=(), joined=True):
        blocks = lax.optimization_barrier(tuple(b for b, _ in sends) + tuple(self.last) + tuple(late))
        came = tuple(move(block) for block, (_, move) in zip(blocks, sends))
        came = lax.optimization_barrier(came) if joined and len(came) > 1 else came
        self.last = came
        return came


def by_core(block):
    return flip(block, 1)


def by_x(block):
    return flip(block, 2)


def by_y(block):
    return flip(block, 4)


def choose(index, options):
    result = options[0]
    for i, option in enumerate(options[1:], 1):
        result = jnp.where(index == i, option, result)
    return result


def by_difference(blocks, index):
    count = len(blocks)
    return [choose(index ^ i, [blocks[d] for d in range(count)]) for i in range(count)]


def group_scatter(block, group_index):
    groups = lax.axis_size("grp")
    size = block.shape[0] // groups
    up = down = None
    for step in range(1, groups):
        goes_up = cut(block, jnp.minimum(groups - step + group_index, groups - 1), size, 0)
        goes_down = cut(block, jnp.maximum(step - groups + group_index, 0), size, 0)
        if up is not None:
            goes_up = (goes_up.astype(F32) + up.astype(F32)).astype(BF16)
            goes_down = (goes_down.astype(F32) + down.astype(F32)).astype(BF16)
        goes_up, goes_down = lax.optimization_barrier((goes_up.astype(BF16), goes_down.astype(BF16)))
        up = lax.ppermute(goes_up, "grp", [(p, p + 1) for p in range(step)])
        down = lax.ppermute(goes_down, "grp", [(groups - 1 - p, groups - 2 - p) for p in range(step)])
        up, down = lax.optimization_barrier((up, down))
    return cut(block, group_index, size, 0).astype(F32) + up.astype(F32) + down.astype(F32)


def small_sum(block):
    for axis in ("seq", "grp"):
        devices, bit = lax.axis_size(axis), 1
        while bit < devices:
            block = block + lax.ppermute(block, axis, [(i, i ^ bit) for i in range(devices)])
            bit *= 2
    return block


def layer_norm(values, gain, bias):
    center = values - jnp.mean(values, axis=-1, keepdims=True)
    spread = jnp.mean(center * center, axis=-1, keepdims=True)
    return center * lax.rsqrt(spread + EPSILON) * gain + bias


def document_table(doc_lengths, positions):
    ends = jnp.cumsum(doc_lengths, dtype=jnp.int32)
    after = (positions[:, None] >= ends[None, :]).astype(jnp.int32)
    documents = jnp.sum(after, axis=1, dtype=jnp.int32)
    starts = jnp.sum(after * doc_lengths[None, :], axis=1, dtype=jnp.int32)
    return (documents, positions - starts)


def rotary_table(places, width):
    half = width // 2
    freqs = 10000.0 ** (-jnp.arange(half, dtype=F32) / (half - 1))
    angles = places.astype(F32)[:, None] * freqs[None, :]
    return jnp.cos(angles), jnp.sin(angles)


def rotate(values, cosine, sine):
    half = values.shape[-1] // 2
    low, high = values[:, :half], values[:, half:]
    return jnp.concatenate([low * cosine - high * sine, high * cosine + low * sine], axis=1)


def rotate_back(grads, cosine, sine):
    return rotate(grads, cosine, -sine)


def decay_mask(query_pos, key_pos, query_doc, key_doc, log_decay, window):
    distance = query_pos[:, None] - key_pos[None, :]
    inside = (distance >= 0) & (query_doc[:, None] == key_doc[None, :]) & (key_pos[None, :] >= 0)
    inside = inside & (distance < window)
    steps = jnp.where(inside, distance, 0).astype(F32)
    return jnp.where(inside, jnp.exp(steps * log_decay), 0.0)


def gate_norm(retained, gate_pre, gain, bias):
    center = retained - jnp.mean(retained, axis=-1, keepdims=True)
    spread = jnp.mean(center * center, axis=-1, keepdims=True)
    grouped = center * lax.rsqrt(spread + EPSILON) * gain + bias
    return jax.nn.silu(gate_pre) * grouped
def body(
    tokens,
    first_gain,
    first_bias,
    query_weight,
    key_weight,
    value_weight,
    gate_weight,
    group_gain,
    group_bias,
    out_weight,
    second_gain,
    second_bias,
    up_weight,
    up_bias,
    down_weight,
    down_bias,
    cotangent,
    doc_lengths,
    windows,
):
    devices, groups = lax.axis_size("seq"), lax.axis_size("grp")
    seq_index, group_index = lax.axis_index("seq"), lax.axis_index("grp")
    chips, quads = devices // 2, devices // 4
    core, chip = seq_index % 2, seq_index // 2
    quarter, quad = seq_index % 4, seq_index // 4
    own_rows, width = tokens.shape
    part = width // devices
    rows = own_rows * groups
    pair_rows = 2 * rows
    ff = up_weight.shape[1]
    ff_part, ff_quarter = ff // devices, ff // 4
    small_mesh = devices == 8
    stages = Stages()

    def head_columns(j):
        return jnp.concatenate(
            [
                cut(query_weight, j, KD, 1),
                cut(key_weight, j, KD, 1),
                cut(value_weight, j, VD, 1),
                cut(gate_weight, j, VD, 1),
            ],
            axis=1,
        )

    mine = head_columns(core)
    theirs = by_core(head_columns(1 - core))
    low_rows = jnp.where(core == 0, mine, theirs)
    high_rows = jnp.where(core == 0, theirs, mine)
    columns = mine.shape[1]

    small = [first_gain, first_bias, second_gain, second_bias, down_bias, up_bias]
    small += [group_gain.T.reshape(-1), group_bias.T.reshape(-1)]
    sizes = [item.shape[0] for item in small]
    packed = lax.all_gather(after(jnp.concatenate(small)[None], theirs), "seq", axis=0, tiled=True).astype(F32)
    whole, start = [], 0
    for size in sizes:
        whole.append(packed[:, start : start + size])
        start += size
    gain_one, bias_one, gain_two, bias_two, down_bias_full, up_bias_full = (
        item.reshape(-1) for item in whole[:6]
    )
    group_gain_f, group_bias_f = (
        pick(item.reshape(devices, 2, -1), core, 1).reshape(1, VD) for item in whole[6:]
    )
    up_bias_quarter = pick(up_bias_full.reshape(quads, 4, ff_part), quarter, 1).reshape(1, ff_quarter)

    inputs = tokens.astype(F32)
    normed = layer_norm(inputs, gain_one, bias_one).astype(BF16)
    gathered = lax.all_gather(normed, "grp", axis=0, tiled=True)

    def join_chips(low, high):
        held = {0: jnp.stack([low, high])}
        for bit in range(1, devices.bit_length() - 1):
            held.update({d | (1 << (bit - 1)): flip(v, 1 << bit) for d, v in list(held.items())})
        return {d: (v[0], v[1]) for d, v in held.items()}

    def quarter_columns(q):
        return [
            lax.dynamic_slice_in_dim(up_weight, (q + 4 * m) * ff_part, ff_part, 1) for m in range(quads)
        ]

    up_sent = jnp.concatenate(quarter_columns(quarter ^ 2) + quarter_columns(quarter ^ 3), axis=1)
    if small_mesh:
        half_low = VD // 2
        out_low, out_high = out_weight[:half_low], out_weight[half_low:]
        low_x, high_y = stages.run((low_rows, by_x), (high_rows, by_y))
        high_xy, low_xy = stages.run(
            (jnp.stack([high_rows, high_y]), by_x), (jnp.stack([low_rows, low_x]), by_y)
        )
        head_held = {
            0: (low_rows, high_rows),
            1: (low_x, high_xy[0]),
            2: (low_xy[0], high_y),
            3: (low_xy[1], high_xy[1]),
        }
        two_x, down_y = stages.run((jnp.stack([up_sent, cotangent]), by_x), (down_weight, by_y))
        up_x, cotangent_x = two_x[0], two_x[1]
        gathered = after(gathered, two_x)
    else:
        head_held = join_chips(low_rows, high_rows)
        up_x = by_x(up_sent)
    head_weight = jnp.zeros((chips, 2, part, columns), BF16)
    for d, (low, high) in head_held.items():
        head_weight = put(head_weight, jnp.stack([low, high])[None], chip ^ d, 0)
    head_weight = head_weight.reshape(width, columns)

    up_core = by_core(
        jnp.stack([jnp.concatenate(quarter_columns(quarter ^ 1), axis=1), up_x[:, ff_quarter:]])
    )
    up_own = jnp.concatenate(quarter_columns(quarter), axis=1)
    up_four = jnp.stack([up_own, up_core[0], up_x[:, :ff_quarter], up_core[1]])

    beside = by_core(gathered)
    pair_normed = jnp.concatenate(
        [jnp.where(core == 0, gathered, beside), jnp.where(core == 0, beside, gathered)], axis=0
    )

    base = chip * pair_rows
    positions = base + jnp.arange(pair_rows, dtype=jnp.int32)
    documents, places = document_table(doc_lengths, positions)
    key_positions = base - rows + jnp.arange(3 * rows, dtype=jnp.int32)
    key_documents = document_table(doc_lengths, key_positions)[0]
    cosine, sine = rotary_table(places, KD)
    key_scale = KD ** (-0.5)
    key_pre = dot(pair_normed, head_weight[:, KD : 2 * KD])
    keys = (rotate(key_pre, cosine, sine) * key_scale).astype(BF16)
    values = dot(pair_normed, head_weight[:, 2 * KD : 2 * KD + VD]).astype(BF16)
    halo = jnp.concatenate([keys[rows:], values[rows:]], axis=1)
    if small_mesh:
        (halo,) = stages.run((halo, lambda v: hop(v, 2)))
    else:
        halo = hop(halo, 2)
    query_pre = dot(pair_normed, head_weight[:, :KD])
    gate_pre = dot(pair_normed, head_weight[:, 2 * KD + VD :])
    queries = rotate(query_pre, cosine, sine).astype(BF16)
    prior_keys, prior_values = halo[:, :KD], halo[:, KD:]

    def key_span(start):
        own = keys[max(start - rows, 0) : start + STRETCH]
        return own if start >= rows else jnp.concatenate([prior_keys[start:], own], axis=0)

    def value_span(start):
        own = values[max(start - rows, 0) : start + STRETCH]
        return own if start >= rows else jnp.concatenate([prior_values[start:], own], axis=0)

    head_index = (group_index * 2 + core).astype(F32)
    log_decay = jnp.log1p(-jnp.exp2(-5.0 - head_index))
    window = windows[0]
    span = rows + STRETCH

    def block_mask(start):
        return decay_mask(
            positions[start : start + STRETCH],
            key_positions[start : start + span],
            documents[start : start + STRETCH],
            key_documents[start : start + span],
            log_decay,
            window,
        )

    pieces = {}
    for start in reversed(range(0, pair_rows, STRETCH)):
        scores = dot(queries[start : start + STRETCH], key_span(start), ((1,), (1,)))
        weights = (scores * block_mask(start)).astype(BF16)
        pieces[start] = dot(weights, value_span(start))
    retained = jnp.concatenate([pieces[start] for start in sorted(pieces)], axis=0)
    heads_out = gate_norm(retained, gate_pre, group_gain_f, group_bias_f).astype(BF16)

    if small_mesh:
        out_low_x, out_high_y = stages.run((out_low, by_x), (out_high, by_y), late=(pieces[rows],))
        out_high_xy, out_low_xy = stages.run(
            (jnp.stack([out_high, out_high_y]), by_x), (jnp.stack([out_low, out_low_x]), by_y)
        )
        out_held = {
            0: (out_low, out_high),
            1: (out_low_x, out_high_xy[0]),
            2: (out_low_xy[0], out_high_y),
            3: (out_low_xy[1], out_high_xy[1]),
        }
        out_head = jnp.zeros((chips, 2, half_low, width), BF16)
        for d, (low, high) in out_held.items():
            out_head = put(out_head, jnp.stack([low, high])[None], chip ^ d, 0)
        out_head = out_head.reshape(groups * VD, width)
    else:
        out_head = lax.all_gather(out_weight, "seq", axis=0, tiled=True)
        out_head = pick(out_head.reshape(groups, 2, VD, width), core, 1).reshape(groups * VD, width)
    up_held, down_held = {0: up_four}, {0: down_weight}
    if small_mesh:
        (up_held[1],) = stages.run((up_four, by_y))
        down_held[1] = down_y
    else:
        for bit in range(2, devices.bit_length() - 1):
            for held in (up_held, down_held):
                held.update({d | (1 << (bit - 2)): flip(v, 1 << bit) for d, v in list(held.items())})
    up_quarter = jnp.zeros((devices, part, ff_quarter), BF16)
    for e, four in up_held.items():
        for d in range(4):
            up_quarter = put(up_quarter, four[d : d + 1], seq_index ^ (4 * e + d), 0)
    up_quarter = up_quarter.reshape(width, ff_quarter)
    down_quarter = jnp.concatenate(by_difference(down_held, quad), axis=0)

    def with_core(two):
        return jnp.concatenate([two, by_core(two)], axis=0)

    def quad_rows(block):
        return with_core(jnp.concatenate([block, by_x(block)], axis=0))

    def quad_sum(block):
        two = block[: 2 * own_rows] + by_core(block[2 * own_rows :].astype(BF16)).astype(F32)
        return two[:own_rows] + by_x(two[own_rows:].astype(BF16)).astype(F32)

    if small_mesh:
        quad_cotangent = with_core(jnp.concatenate([cotangent, cotangent_x], axis=0))
    else:
        quad_cotangent = quad_rows(cotangent)

    def to_tokens(block):
        parted = block.reshape(2, groups, own_rows, VD)
        result = jnp.zeros((2 * own_rows, groups * VD), BF16)
        for by in range(groups):
            sent = pick(parted, (group_index + by) % groups, 1).reshape(2 * own_rows, VD)
            result = put(result, turn(sent, by) if by else sent, (group_index - by) % groups, 1)
        return result

    def to_heads(block):
        result = jnp.zeros((2, groups, own_rows, VD), BF16)
        for by in range(groups):
            sent = cut(block, (group_index + by) % groups, VD, 1)
            came = turn(sent, by) if by else sent
            result = put(result, came.reshape(2, 1, own_rows, VD), (group_index - by) % groups, 1)
        return result.reshape(pair_rows, VD)

    def pair_sum(block, size, kind):
        mine = cut(block, core, size, 0)
        return mine + by_core(cut(block, 1 - core, size, 0).astype(kind)).astype(F32)

    def pair_rows_of(block):
        beside = by_core(block)
        return jnp.concatenate(
            [jnp.where(core == 0, block, beside), jnp.where(core == 0, beside, block)], axis=0
        )

    by_token = to_tokens(heads_out)
    hidden = inputs + pair_sum(dot(by_token, out_head), own_rows, F32)
    normed_two = layer_norm(hidden, gain_two, bias_two).astype(BF16)
    quad_normed = quad_rows(normed_two)
    pre_act = dot(quad_normed, up_quarter) + up_bias_quarter
    activated = jax.nn.gelu(pre_act, approximate=False).astype(BF16)

    grad_out = cotangent.astype(F32)
    down_bias_part = jnp.sum(grad_out, axis=0)
    grad_act = dot(quad_cotangent, down_quarter, ((1,), (1,)))
    gelu_back = jax.vjp(partial(jax.nn.gelu, approximate=False), pre_act)[1]
    grad_pre = gelu_back(grad_act)[0].astype(BF16)
    up_bias_part = jnp.sum(grad_pre.astype(F32), axis=0)
    down_part = dot(activated, quad_cotangent, ((0,), (0,))).astype(BF16).reshape(quads, ff_part, width)
    two_part = dot(grad_pre, up_quarter, ((1,), (1,)))
    if small_mesh:
        two = two_part[: 2 * own_rows] + by_core(two_part[2 * own_rows :].astype(BF16)).astype(F32)
        two_x, down_y = stages.run(
            (two[own_rows:].astype(BF16), by_x), (pick(down_part, 1 - quad), by_y), joined=False
        )
        grad_normed_two = two[:own_rows] + two_x.astype(F32)
    else:
        grad_normed_two = quad_sum(two_part)
    second_back = jax.vjp(layer_norm, hidden, gain_two, bias_two)[1]
    hidden_part, gain_two_part, bias_two_part = second_back(grad_normed_two)
    grad_hidden = grad_out + hidden_part
    grad_attend = pair_rows_of(grad_hidden.astype(BF16))
    grad_by_token = dot(grad_attend, out_head, ((1,), (1,))).astype(BF16)
    grad_heads = to_heads(grad_by_token)

    up_part = dot(quad_normed, grad_pre, ((0,), (0,))).astype(BF16).reshape(quads, 4, part, ff_quarter)
    out_part = dot(by_token, grad_attend, ((0,), (0,))).astype(BF16)

    def split_chips(parts):
        held, bit = dict(parts), 1
        while bit < chips:
            sent = {d: flip(v.astype(BF16), 2 * bit) for d, v in held.items() if d & bit}
            held = {
                d: v.astype(F32) + sent[d | bit].astype(F32) for d, v in held.items() if not d & bit
            }
            bit *= 2
        return held[0]

    def split_quads(block):
        held, bit = {d: pick(block, quad ^ d) for d in range(quads)}, 1
        while bit < quads:
            sent = {d: flip(v.astype(BF16), 4 * bit) for d, v in held.items() if d & bit}
            held = {
                d: v.astype(F32) + sent[d | bit].astype(F32) for d, v in held.items() if not d & bit
            }
            bit *= 2
        return held[0]

    def plus(mine, came):
        return mine.astype(F32) + came.astype(F32)

    def up_to_owners(up_four, up_x):
        up_core = by_core(jnp.stack([pick(up_four, quarter ^ 1), up_x[1]]))
        up_blocks = by_difference([pick(up_four, quarter), up_core[0], up_x[0], up_core[1]], quarter)
        return jnp.concatenate(
            [block[:, m * ff_part : (m + 1) * ff_part] for m in range(quads) for block in up_blocks], axis=1
        )

    def up_x_sent(up_four):
        return jnp.stack([pick(up_four, quarter ^ 2), pick(up_four, quarter ^ 3)])

    mixed_part = dot(activated, down_quarter)
    if small_mesh:
        mixed_two = plus(mixed_part[: 2 * own_rows], by_core(mixed_part[2 * own_rows :].astype(BF16)))
        down_sum = plus(pick(down_part, quad), down_y).astype(BF16)
        out_part = out_part.reshape(chips, 2, half_low, width)
        low, high = ([pick(out_part[:, i], chip ^ d) for d in range(chips)] for i in (0, 1))
        high_x, up_y = stages.run(
            (jnp.stack([high[1], high[3]]), by_x), (pick(up_part, 1 - quad), by_y), late=(grad_by_token,)
        )
        up_four = plus(pick(up_part, quad), up_y).astype(BF16)
        up_x, low_y = stages.run(
            (up_x_sent(up_four), by_x), (jnp.stack([low[2], low[3]]), by_y), late=(grad_heads,)
        )
    else:
        mixed_sum = quad_sum(mixed_part)
        down_sum = split_quads(down_part).astype(BF16)
        up_four = split_quads(up_part).astype(BF16)
        up_x = by_x(up_x_sent(up_four))
        spread = jnp.zeros((groups, 2, VD, width), BF16)
        spread = put(spread, out_part.reshape(groups, 1, VD, width), core, 1)
        out_sum = lax.psum_scatter(
            spread.reshape(groups * 2 * VD, width), "seq", scatter_dimension=0, tiled=True
        )
    up_sum = up_to_owners(up_four, up_x)
    down_sum = lax.psum(after(down_sum, grad_heads), "grp")
    gate_back = jax.vjp(gate_norm, retained, gate_pre, group_gain_f, group_bias_f)[1]
    grad_retained, grad_gate, group_gain_part, group_bias_part = gate_back(grad_heads.astype(F32))
    grad_retained = grad_retained.astype(BF16)
    grad_gate = grad_gate.astype(BF16)
    key_sums = jnp.zeros((3 * rows, KD), F32)
    value_sums = jnp.zeros((3 * rows, VD), F32)
    query_parts = []
    for start in range(0, pair_rows, STRETCH):
        mask = block_mask(start)
        block_queries = queries[start : start + STRETCH]
        block_keys, block_values = key_span(start), value_span(start)
        block_grad = grad_retained[start : start + STRETCH]
        weights = (dot(block_queries, block_keys, ((1,), (1,))) * mask).astype(BF16)
        grad_scores = (dot(block_grad, block_values, ((1,), (1,))) * mask).astype(BF16)
        value_sums = value_sums.at[start : start + span].add(dot(weights, block_grad, ((0,), (0,))))
        key_sums = key_sums.at[start : start + span].add(dot(grad_scores, block_queries, ((0,), (0,))))
        query_parts.append(dot(grad_scores, block_keys))
    grad_queries = jnp.concatenate(query_parts, axis=0)
    later = jnp.concatenate([key_sums[:rows], value_sums[:rows]], axis=1).astype(BF16)
    if small_mesh:
        (later,) = stages.run((later, lambda v: hop(v, -2)))
        low_x, high_y = stages.run(
            (plus(low[1], low_y[1]).astype(BF16), by_x), (plus(high[2], high_x[1]).astype(BF16), by_y)
        )
        low_sum = plus(plus(low[0], low_y[0]), low_x)
        high_sum = plus(plus(high[0], high_x[0]), high_y)
        out_sum = jnp.concatenate([low_sum, high_sum], axis=0)
    else:
        later = hop(later, -2)
    up_sum = lax.psum(after(up_sum, down_sum), "grp")
    out_sum = lax.psum(after(out_sum.astype(BF16), up_sum), "grp")
    down_grad, up_grad, out_grad = down_sum.astype(F32), up_sum.astype(F32), out_sum.astype(F32)

    own_keys = key_sums[rows:].at[rows:].add(later[:, :KD].astype(F32))
    grad_values = value_sums[rows:].at[rows:].add(later[:, KD:].astype(F32)).astype(BF16)
    grad_query = rotate_back(grad_queries, cosine, sine).astype(BF16)
    grad_key = (rotate_back(own_keys, cosine, sine) * key_scale).astype(BF16)
    grads = jnp.concatenate([grad_query, grad_key, grad_values, grad_gate], axis=1)

    normed_part = pair_sum(dot(grads, head_weight, ((1,), (1,))), rows, BF16)
    grad_normed = group_scatter(normed_part, group_index)
    head_part = dot(pair_normed, grads, ((0,), (0,)))
    product_part = jnp.sum(head_part * head_weight.astype(F32), axis=1)
    bias_one_part = jnp.sum(head_weight.astype(F32) * jnp.sum(grads.astype(F32), axis=0)[None], axis=1)
    gain_one_part = (product_part - bias_one * bias_one_part) / gain_one
    head_part = head_part.astype(BF16).reshape(chips, 2, part, columns)
    parts = {d: pick(head_part, chip ^ d) for d in range(chips)}
    if small_mesh:
        high_x, low_y = stages.run(
            (jnp.stack([parts[1][1], parts[3][1]]), by_x), (jnp.stack([parts[2][0], parts[3][0]]), by_y)
        )
        low_x, high_y = stages.run(
            (plus(parts[1][0], low_y[1]).astype(BF16), by_x),
            (plus(parts[2][1], high_x[1]).astype(BF16), by_y),
        )
        (mixed_x,) = stages.run((mixed_two[own_rows:].astype(BF16), by_x))
        mixed_sum = plus(mixed_two[:own_rows], mixed_x)
        low_sum = plus(plus(parts[0][0], low_y[0]), low_x)
        high_sum = plus(plus(parts[0][1], high_x[0]), high_y)
    else:
        low_sum, high_sum = split_chips(parts)
    mixed = (hidden + mixed_sum + down_bias_full).astype(BF16)
    own_head = jnp.where(core == 0, low_sum, high_sum)
    other_head = by_core(jnp.where(core == 0, high_sum, low_sum).astype(BF16)).astype(F32)
    first_head = jnp.where(core == 0, own_head, other_head)
    second_head = jnp.where(core == 0, other_head, own_head)

    def both_heads(start, size):
        return jnp.concatenate(
            [first_head[:, start : start + size], second_head[:, start : start + size]], axis=1
        )

    query_grad, key_grad = both_heads(0, KD), both_heads(KD, KD)
    value_grad, gate_grad = both_heads(2 * KD, VD), both_heads(2 * KD + VD, VD)

    up_bias_whole = put(jnp.zeros((quads, 4, ff_part), F32), up_bias_part.reshape(quads, 1, ff_part), quarter, 1)
    group_whole = jnp.zeros((groups, 2, 2, VD), F32)
    group_pair = jnp.stack([group_gain_part.reshape(-1), group_bias_part.reshape(-1)])
    group_whole = lax.dynamic_update_slice(group_whole, group_pair[None, None], (group_index, core, 0, 0))
    group_rows = group_whole.reshape(groups, 4, devices, VD // devices).transpose(2, 0, 1, 3)
    pieces = [
        item.reshape(devices, -1)
        for item in (
            gain_one_part,
            bias_one_part,
            gain_two_part,
            bias_two_part,
            down_bias_part,
            up_bias_whole,
            group_rows,
        )
    ]
    sums = small_sum(jnp.concatenate(pieces, axis=1))
    sums = pick(sums, seq_index)
    first_back = jax.vjp(lambda v: layer_norm(v, gain_one, bias_one), inputs)[1]
    tokens_grad = (grad_hidden + first_back(after(grad_normed, sums))[0]).astype(BF16)
    taken, start = [], 0
    for item in pieces:
        taken.append(sums[start : start + item.shape[1]])
        start += item.shape[1]
    first_gain_grad, first_bias_grad, second_gain_grad, second_bias_grad = taken[:4]
    down_bias_grad, up_bias_grad = taken[4:6]
    group_own = pick(taken[6].reshape(groups, 2, 2, VD // devices), group_index)
    group_gain_grad, group_bias_grad = group_own[:, 0].T, group_own[:, 1].T
    return (
        mixed,
        tokens_grad,
        first_gain_grad,
        first_bias_grad,
        query_grad,
        key_grad,
        value_grad,
        gate_grad,
        group_gain_grad,
        group_bias_grad,
        out_grad,
        second_gain_grad,
        second_bias_grad,
        up_grad,
        up_bias_grad,
        down_grad,
        down_bias_grad,
    )


def solution(mesh):
    placed = (
        P(("seq", "grp"), None),
        P("seq"),
        P("seq"),
        P("seq", "grp"),
        P("seq", "grp"),
        P("seq", "grp"),
        P("seq", "grp"),
        P("seq", "grp"),
        P("seq", "grp"),
        P("seq", None),
        P("seq"),
        P("seq"),
        P("seq", None),
        P("seq"),
        P("seq", None),
        P("seq"),
        P(("seq", "grp"), None),
        P(),
        P("grp"),
    )
    return jax.shard_map(
        body,
        mesh=mesh,
        in_specs=placed,
        out_specs=(
            P(("seq", "grp"), None),
            P(("seq", "grp"), None),
            P("seq"),
            P("seq"),
            P("seq", "grp"),
            P("seq", "grp"),
            P("seq", "grp"),
            P("seq", "grp"),
            P("seq", "grp"),
            P("seq", "grp"),
            P("seq", None),
            P("seq"),
            P("seq"),
            P("seq", None),
            P("seq"),
            P("seq", None),
            P("seq"),
        ),
        check_vma=False,
    )
```

```python
import jax
import jax.numpy as jnp
from jax import lax
from jax.experimental import pallas as pl
from jax.experimental.pallas import tpu as pltpu
from jax.sharding import PartitionSpec as P

KD = 256
VD = 512
TILE = 256
VMEM_LIMIT = 48 * 2**20
EPSILON = 1e-05

F32 = jnp.float32
BF16 = jnp.bfloat16


def dot(a, b, dims=((1,), (0,))):
    return lax.dot_general(a, b, (dims, ((), ())), preferred_element_type=F32)


def flip(block, bit):
    devices = lax.axis_size("seq")
    return lax.ppermute(block, "seq", [(i, i ^ bit) for i in range(devices)])


def hop(block, by):
    devices = lax.axis_size("seq")
    return lax.ppermute(block, "seq", [(i, i + by) for i in range(devices) if 0 <= i + by < devices])


def turn(block, by):
    groups = lax.axis_size("grp")
    return lax.ppermute(block, "grp", [(i, (i + by) % groups) for i in range(groups)])


def pick(array, index, axis=0):
    return lax.dynamic_index_in_dim(array, index, axis, keepdims=False)


def cut(array, index, size, axis):
    return lax.dynamic_slice_in_dim(array, index * size, size, axis)


def put(array, block, index, axis):
    return lax.dynamic_update_slice_in_dim(array, block, index * block.shape[axis], axis)


def after(block, *others):
    return lax.optimization_barrier((block, *others))[0]


class Stages:
    def __init__(self):
        self.last = ()

    def run(self, *sends, late=(), chain=None, joined=True):
        first = tuple(self.last if chain is None else chain) + tuple(late)
        blocks = lax.optimization_barrier(tuple(b for b, _ in sends) + first)
        came = tuple(move(block) for block, (_, move) in zip(blocks, sends))
        came = lax.optimization_barrier(came) if joined and len(came) > 1 else came
        self.last = came
        return came


def by_core(block):
    return flip(block, 1)


def by_x(block):
    return flip(block, 2)


def by_y(block):
    return flip(block, 4)


def choose(index, options):
    result = options[0]
    for i, option in enumerate(options[1:], 1):
        result = jnp.where(index == i, option, result)
    return result


def by_difference(blocks, index):
    count = len(blocks)
    return [choose(index ^ i, [blocks[d] for d in range(count)]) for i in range(count)]


class GroupLine:
    def __init__(self, group_index, count):
        self.groups = lax.axis_size("grp")
        self.index, self.count = group_index, count
        self.pieces = {}
        self.came = {"up": [], "down": []}

    def add(self, *pieces):
        for piece in lax.optimization_barrier(pieces):
            self.pieces[len(self.pieces)] = (piece, piece)

    def add_blocks(self, blocks):
        blocks = lax.optimization_barrier(tuple(blocks))
        for i in range(self.groups - 1):
            self.pieces[self.count + i] = (blocks[self.groups - 1 - i], blocks[i])

    def step(self, *late):
        step, groups = len(self.came["up"]), self.groups
        sends = []
        for way, place in (("up", self.index), ("down", groups - 1 - self.index)):
            side = 0 if way == "up" else 1
            pairs, options = [], []
            for p in range(groups - 1):
                item = step - p
                ahead = item - self.count
                live = item in self.pieces and (ahead < 0 or p + 1 <= groups - 1 - ahead)
                if live:
                    pairs.append((p, p + 1) if side == 0 else (groups - 1 - p, groups - 2 - p))
                options.append(self.pieces[item][side] if live else None)
            known = next(option for option in options if option is not None)
            sent = choose(place, [known if option is None else option for option in options])
            if step:
                sent = (sent.astype(F32) + self.came[way][-1].astype(F32)).astype(BF16)
            sends.append((sent, pairs))
        blocks = lax.optimization_barrier(tuple(sent for sent, _ in sends) + late)
        for way, block, (_, pairs) in zip(("up", "down"), blocks, sends):
            self.came[way].append(lax.ppermute(block, "grp", pairs))

    def total(self, item):
        groups = self.groups
        piece = self.pieces[item][0]
        zero = jnp.zeros_like(piece)
        below = choose(self.index, [zero] + self.came["up"][item : item + groups - 1])
        above = choose(groups - 1 - self.index, [zero] + self.came["down"][item : item + groups - 1])
        return piece.astype(F32) + below.astype(F32) + above.astype(F32)

    def last(self):
        step = self.count + self.groups - 2
        return self.came["up"][step].astype(F32) + self.came["down"][step].astype(F32)


def small_sum(block):
    for axis in ("seq", "grp"):
        devices, bit = lax.axis_size(axis), 1
        while bit < devices:
            block = block + lax.ppermute(block, axis, [(i, i ^ bit) for i in range(devices)])
            bit *= 2
    return block


def layer_norm(values, gain, bias):
    center = values - jnp.mean(values, axis=-1, keepdims=True)
    spread = jnp.mean(center * center, axis=-1, keepdims=True)
    return center * lax.rsqrt(spread + EPSILON) * gain + bias


def document_table(doc_lengths, positions):
    ends = jnp.cumsum(doc_lengths, dtype=jnp.int32)
    after = (positions[:, None] >= ends[None, :]).astype(jnp.int32)
    documents = jnp.sum(after, axis=1, dtype=jnp.int32)
    starts = jnp.sum(after * doc_lengths[None, :], axis=1, dtype=jnp.int32)
    return (documents, positions - starts)


def rotary_table(places, width):
    half = width // 2
    freqs = 10000.0 ** (-jnp.arange(half, dtype=F32) / (half - 1))
    angles = places.astype(F32)[:, None] * freqs[None, :]
    return jnp.cos(angles), jnp.sin(angles)


def rotate(values, cosine, sine):
    half = values.shape[-1] // 2
    low, high = values[:, :half], values[:, half:]
    return jnp.concatenate([low * cosine - high * sine, high * cosine + low * sine], axis=1)


def rotate_back(grads, cosine, sine):
    return rotate(grads, cosine, -sine)


def tile_bounds(starts_ref, window, first, rows, axis):
    shape = (rows, 1) if axis == 0 else (1, rows)
    position = first + lax.broadcasted_iota(jnp.int32, shape, axis)
    earliest = jnp.maximum(position - window + 1, 0)
    for d in range(starts_ref.shape[0]):
        begin = starts_ref[d]
        earliest = jnp.where(position >= begin, jnp.maximum(earliest, begin), earliest)
    return position, earliest


def retention_kernel(
    place_ref,
    starts_ref,
    decay_ref,
    query_ref,
    key_low_ref,
    key_high_ref,
    value_low_ref,
    value_high_ref,
    gate_ref,
    gain_ref,
    bias_ref,
    out_ref,
    hat_ref,
    scale_ref,
):
    half = key_low_ref.shape[0]
    log_decay = decay_ref[0]
    for tile in range(query_ref.shape[0] // TILE):
        begin = tile * TILE
        first = place_ref[0] + begin
        rows = slice(begin, begin + TILE)
        position, earliest = tile_bounds(starts_ref, place_ref[1], first, TILE, 0)
        row_decay = jnp.exp((position - first).astype(F32) * log_decay)
        total = jnp.zeros((TILE, VD), F32)
        for keys, values, low, high, offset in (
            (key_low_ref, value_low_ref, begin, half, begin - half),
            (key_high_ref, value_high_ref, 0, begin + TILE, begin * 0),
        ):
            count = high - low
            ahead = (low - begin) - (half if keys is key_low_ref else 0)
            column = first + ahead + lax.broadcasted_iota(jnp.int32, (1, count), 1)
            column_decay = jnp.exp((first - column).astype(F32) * log_decay)
            scores = dot(query_ref[rows, :], keys[low:high, :], ((1,), (1,)))
            inside = (column <= position) & (column >= earliest)
            weights = jnp.where(inside, scores * (row_decay * column_decay), 0.0).astype(BF16)
            total = total + dot(weights, values[low:high, :])
        center = total - jnp.mean(total, axis=1, keepdims=True)
        scale = lax.rsqrt(jnp.mean(center * center, axis=1, keepdims=True) + EPSILON)
        hat = center * scale
        gate = gate_ref[rows, :].astype(F32)
        silu = gate / (1.0 + jnp.exp(-gate))
        out_ref[rows, :] = (silu * (hat * gain_ref[...] + bias_ref[...])).astype(BF16)
        hat_ref[rows, :] = hat.astype(BF16)
        scale_ref[rows, :] = jnp.broadcast_to(scale, (TILE, 128))


def retention_back_kernel(
    place_ref,
    starts_ref,
    decay_ref,
    query_ref,
    key_low_ref,
    key_high_ref,
    value_low_ref,
    value_high_ref,
    gate_ref,
    gain_ref,
    bias_ref,
    hat_ref,
    scale_ref,
    grad_ref,
    query_grad_ref,
    gate_grad_ref,
    low_grad_ref,
    high_grad_ref,
    gain_grad_ref,
    bias_grad_ref,
):
    half = key_low_ref.shape[0]
    log_decay = decay_ref[0]
    gain, bias = gain_ref[...], bias_ref[...]
    gain_grad = jnp.zeros((1, VD), F32)
    bias_grad = jnp.zeros((1, VD), F32)
    low_grad_ref[...] = jnp.zeros_like(low_grad_ref)
    high_grad_ref[...] = jnp.zeros_like(high_grad_ref)
    for tile in range(query_ref.shape[0] // TILE):
        begin = tile * TILE
        first = place_ref[0] + begin
        rows = slice(begin, begin + TILE)
        hat = hat_ref[rows, :].astype(F32)
        grad = grad_ref[rows, :].astype(F32)
        gate = gate_ref[rows, :].astype(F32)
        sigmoid = 1.0 / (1.0 + jnp.exp(-gate))
        silu = gate * sigmoid
        grouped_grad = grad * silu
        gate_grad = grad * (hat * gain + bias) * (sigmoid + silu * (1.0 - sigmoid))
        gate_grad_ref[rows, :] = gate_grad.astype(BF16)
        gain_grad = gain_grad + jnp.sum(grouped_grad * hat, axis=0, keepdims=True)
        bias_grad = bias_grad + jnp.sum(grouped_grad, axis=0, keepdims=True)
        inner = grouped_grad * gain
        mean = jnp.mean(inner, axis=1, keepdims=True)
        along = jnp.mean(inner * hat, axis=1, keepdims=True)
        kept_grad = ((inner - mean - hat * along) * scale_ref[rows, :1]).astype(BF16)
        query = query_ref[rows, :]
        position, earliest = tile_bounds(starts_ref, place_ref[1], first, TILE, 1)
        row_decay = jnp.exp((position - first).astype(F32) * log_decay)
        query_grad = jnp.zeros((TILE, KD), F32)
        for keys, values, sums, low, high in (
            (key_low_ref, value_low_ref, low_grad_ref, begin, half),
            (key_high_ref, value_high_ref, high_grad_ref, 0, begin + TILE),
        ):
            count = high - low
            ahead = (low - begin) - (half if keys is key_low_ref else 0)
            column = first + ahead + lax.broadcasted_iota(jnp.int32, (count, 1), 0)
            column_decay = jnp.exp((first - column).astype(F32) * log_decay)
            inside = (column <= position) & (column >= earliest)
            mask = jnp.where(inside, row_decay * column_decay, 0.0)
            key, value = keys[low:high, :], values[low:high, :]
            weights = (dot(key, query, ((1,), (1,))) * mask).astype(BF16)
            scores = (dot(value, kept_grad, ((1,), (1,))) * mask).astype(BF16)
            sums[low:high, KD:] += dot(weights, kept_grad)
            sums[low:high, :KD] += dot(scores, query)
            query_grad = query_grad + dot(scores, key, ((0,), (0,)))
        query_grad_ref[rows, :] = query_grad
    gain_grad_ref[...] = gain_grad
    bias_grad_ref[...] = bias_grad


def whole_spec(*shape):
    return pl.BlockSpec(shape, lambda _: (0,) * len(shape))


def retention_specs(rows, low, high):
    def part(width, index):
        return pl.BlockSpec((rows, width), lambda _: (index, 0))

    smem = pl.BlockSpec(memory_space=pltpu.SMEM)
    return [smem] * 3 + [
        part(KD, high[1]),
        part(KD, low),
        part(KD, high[0]),
        part(VD, low),
        part(VD, high[0]),
        part(VD, high[1]),
        whole_spec(1, VD),
        whole_spec(1, VD),
    ]


def retention(place, starts, decay, queries, keys, values, gate, gain, bias, rows, low, high):
    cost = pl.CostEstimate(flops=rows * 1280 * 192, bytes_accessed=rows * 1024, transcendentals=0)
    return pl.pallas_call(
        retention_kernel,
        out_shape=(
            jax.ShapeDtypeStruct((rows, VD), BF16),
            jax.ShapeDtypeStruct((rows, VD), BF16),
            jax.ShapeDtypeStruct((rows, 128), F32),
        ),
        grid=(1,),
        in_specs=retention_specs(rows, low, high),
        out_specs=(whole_spec(rows, VD), whole_spec(rows, VD), whole_spec(rows, 128)),
        compiler_params=pltpu.CompilerParams(vmem_limit_bytes=VMEM_LIMIT),
        cost_estimate=cost,
    )(place, starts, decay, queries, keys[0], keys[1], values[0], values[1], gate, gain, bias)


def retention_back(
    place, starts, decay, queries, keys, values, gate, gain, bias, hat, scale, grad, rows, low, high
):
    cost = pl.CostEstimate(flops=rows * 1280 * 448, bytes_accessed=rows * 2048, transcendentals=0)
    part = pl.BlockSpec((rows, VD), lambda _: (high[1], 0))
    return pl.pallas_call(
        retention_back_kernel,
        out_shape=(
            jax.ShapeDtypeStruct((rows, KD), F32),
            jax.ShapeDtypeStruct((rows, VD), BF16),
            jax.ShapeDtypeStruct((rows, KD + VD), F32),
            jax.ShapeDtypeStruct((rows, KD + VD), F32),
            jax.ShapeDtypeStruct((1, VD), F32),
            jax.ShapeDtypeStruct((1, VD), F32),
        ),
        grid=(1,),
        in_specs=retention_specs(rows, low, high)
        + [whole_spec(rows, VD), whole_spec(rows, 128), part],
        out_specs=(
            whole_spec(rows, KD),
            whole_spec(rows, VD),
            whole_spec(rows, KD + VD),
            whole_spec(rows, KD + VD),
            whole_spec(1, VD),
            whole_spec(1, VD),
        ),
        compiler_params=pltpu.CompilerParams(vmem_limit_bytes=VMEM_LIMIT),
        cost_estimate=cost,
    )(place, starts, decay, queries, keys[0], keys[1], values[0], values[1], gate, gain, bias, hat, scale, grad)


def feed_kernel(
    normed_ref,
    cotangent_ref,
    up_ref,
    down_ref,
    bias_ref,
    activated_ref,
    grad_pre_ref,
    mixed_ref,
    grad_ref,
    bias_grad_ref,
):
    up, down = up_ref[...], down_ref[...]
    pre = dot(normed_ref[...], up) + bias_ref[...]
    grad_act = dot(cotangent_ref[...], down, ((1,), (1,)))
    share = 0.5 + 0.5 * lax.erf(pre * 0.7071067811865476)
    bell = jnp.exp(-0.5 * pre * pre) * 0.3989422804014327
    activated = (pre * share).astype(BF16)
    grad_pre = (grad_act * (share + pre * bell)).astype(BF16)
    activated_ref[...] = activated
    grad_pre_ref[...] = grad_pre
    mixed_ref[...] = dot(activated, down).astype(BF16)
    grad_ref[...] = dot(grad_pre, up, ((1,), (1,))).astype(BF16)

    @pl.when(pl.program_id(0) == 0)
    def _():
        bias_grad_ref[...] = jnp.zeros_like(bias_grad_ref)

    bias_grad_ref[...] += jnp.sum(grad_pre.astype(F32), axis=0, keepdims=True)


def feed(normed, cotangent, up, down, bias):
    rows, width = normed.shape
    hidden = up.shape[1]

    def tiled(columns):
        return pl.BlockSpec((TILE, columns), lambda i: (i, 0))

    cost = pl.CostEstimate(
        flops=rows * width * hidden, bytes_accessed=rows * width, transcendentals=0
    )
    return pl.pallas_call(
        feed_kernel,
        out_shape=(
            jax.ShapeDtypeStruct((rows, hidden), BF16),
            jax.ShapeDtypeStruct((rows, hidden), BF16),
            jax.ShapeDtypeStruct((rows, width), BF16),
            jax.ShapeDtypeStruct((rows, width), BF16),
            jax.ShapeDtypeStruct((1, hidden), F32),
        ),
        grid=(rows // TILE,),
        in_specs=[
            tiled(width),
            tiled(width),
            whole_spec(*up.shape),
            whole_spec(*down.shape),
            whole_spec(1, hidden),
        ],
        out_specs=(tiled(hidden), tiled(hidden), tiled(width), tiled(width), whole_spec(1, hidden)),
        compiler_params=pltpu.CompilerParams(vmem_limit_bytes=VMEM_LIMIT),
        cost_estimate=cost,
    )(normed, cotangent, up, down, bias)
def body(
    tokens,
    first_gain,
    first_bias,
    query_weight,
    key_weight,
    value_weight,
    gate_weight,
    group_gain,
    group_bias,
    out_weight,
    second_gain,
    second_bias,
    up_weight,
    up_bias,
    down_weight,
    down_bias,
    cotangent,
    doc_lengths,
    windows,
):
    devices, groups = lax.axis_size("seq"), lax.axis_size("grp")
    seq_index, group_index = lax.axis_index("seq"), lax.axis_index("grp")
    chips, quads = devices // 2, devices // 4
    core, chip = seq_index % 2, seq_index // 2
    quarter, quad = seq_index % 4, seq_index // 4
    own_rows, width = tokens.shape
    part = width // devices
    rows = own_rows * groups
    pair_rows = 2 * rows
    ff = up_weight.shape[1]
    ff_part, ff_quarter = ff // devices, ff // 4
    small_mesh = devices == 8
    stages = Stages()

    def head_columns(j):
        return jnp.concatenate(
            [
                cut(query_weight, j, KD, 1),
                cut(key_weight, j, KD, 1),
                cut(value_weight, j, VD, 1),
                cut(gate_weight, j, VD, 1),
            ],
            axis=1,
        )

    mine = head_columns(core)
    theirs = by_core(head_columns(1 - core))
    low_rows = jnp.where(core == 0, mine, theirs)
    high_rows = jnp.where(core == 0, theirs, mine)
    columns = mine.shape[1]

    small = [first_gain, first_bias, second_gain, second_bias, down_bias, up_bias]
    small += [group_gain.T.reshape(-1), group_bias.T.reshape(-1)]
    sizes = [item.shape[0] for item in small]
    packed = lax.all_gather(after(jnp.concatenate(small)[None], low_rows, high_rows), "seq", axis=0, tiled=True).astype(F32)
    whole, start = [], 0
    for size in sizes:
        whole.append(packed[:, start : start + size])
        start += size
    gain_one, bias_one, gain_two, bias_two, down_bias_full, up_bias_full = (
        item.reshape(-1) for item in whole[:6]
    )
    group_gain_f, group_bias_f = (
        pick(item.reshape(devices, 2, -1), core, 1).reshape(1, VD) for item in whole[6:]
    )
    up_bias_quarter = pick(up_bias_full.reshape(quads, 4, ff_part), quarter, 1).reshape(1, ff_quarter)

    inputs = tokens.astype(F32)
    normed = layer_norm(inputs, gain_one, bias_one).astype(BF16)
    gathered = lax.all_gather(normed, "grp", axis=0, tiled=True)

    base = chip * pair_rows
    positions = base + jnp.arange(pair_rows, dtype=jnp.int32)
    places = document_table(doc_lengths, positions)[1]
    doc_starts = jnp.cumsum(doc_lengths, dtype=jnp.int32) - doc_lengths
    cosine, sine = rotary_table(places, KD)
    def join_chips(low, high):
        held = {0: jnp.stack([low, high])}
        for bit in range(1, devices.bit_length() - 1):
            held.update({d | (1 << (bit - 1)): flip(v, 1 << bit) for d, v in list(held.items())})
        return {d: (v[0], v[1]) for d, v in held.items()}

    def quarter_columns(q):
        return [
            lax.dynamic_slice_in_dim(up_weight, (q + 4 * m) * ff_part, ff_part, 1) for m in range(quads)
        ]

    up_sent = jnp.concatenate(quarter_columns(quarter ^ 2) + quarter_columns(quarter ^ 3), axis=1)
    if small_mesh:
        half_low = VD // 2
        out_low, out_high = out_weight[:half_low], out_weight[half_low:]
        low_x, high_y = stages.run((low_rows, by_x), (high_rows, by_y))
        high_xy, low_xy = stages.run(
            (jnp.stack([high_rows, high_y]), by_x), (jnp.stack([low_rows, low_x]), by_y)
        )
        head_held = {
            0: (low_rows, high_rows),
            1: (low_x, high_xy[0]),
            2: (low_xy[0], high_y),
            3: (low_xy[1], high_xy[1]),
        }
        two_x, down_y = stages.run((jnp.stack([up_sent, cotangent]), by_x), (down_weight, by_y))
        up_x, cotangent_x = two_x[0], two_x[1]
        gathered = after(gathered, high_xy, low_xy, cosine, sine)
    else:
        head_held = join_chips(low_rows, high_rows)
        up_x = by_x(up_sent)
    head_weight = jnp.zeros((chips, 2, part, columns), BF16)
    for d, (low, high) in head_held.items():
        head_weight = put(head_weight, jnp.stack([low, high])[None], chip ^ d, 0)
    head_weight = head_weight.reshape(width, columns)

    up_core = by_core(
        jnp.stack([jnp.concatenate(quarter_columns(quarter ^ 1), axis=1), up_x[:, ff_quarter:]])
    )
    up_own = jnp.concatenate(quarter_columns(quarter), axis=1)
    up_four = jnp.stack([up_own, up_core[0], up_x[:, :ff_quarter], up_core[1]])

    beside = by_core(gathered)
    pair_normed = jnp.concatenate(
        [jnp.where(core == 0, gathered, beside), jnp.where(core == 0, beside, gathered)], axis=0
    )

    key_scale = KD ** (-0.5)
    key_pre = dot(pair_normed, head_weight[:, KD : 2 * KD])
    keys = (rotate(key_pre, cosine, sine) * key_scale).astype(BF16)
    values = dot(pair_normed, head_weight[:, 2 * KD : 2 * KD + VD]).astype(BF16)
    halo = jnp.concatenate([keys[rows:], values[rows:]], axis=1)
    if small_mesh:
        weights_last = stages.last
        (halo,) = stages.run((halo, lambda v: hop(v, 2)), chain=(high_xy, low_xy))
    else:
        halo = hop(halo, 2)
    query_pre = dot(pair_normed, head_weight[:, :KD])
    gate_pre = dot(pair_normed, head_weight[:, 2 * KD + VD :]).astype(BF16)
    queries = rotate(query_pre, cosine, sine).astype(BF16)
    halo = (halo[:, :KD], halo[:, KD:])
    head_index = (group_index * 2 + core).astype(F32)
    log_decay = jnp.log1p(-jnp.exp2(-5.0 - head_index)).reshape(1)
    window = windows[0]

    shared = (doc_starts, log_decay, queries)
    late_rows, early_rows = (0, (1, 1)), (0, (0, 0))
    late_place = jnp.stack([base + rows, window])
    early_place = jnp.stack([base, window])
    late_keys, late_values = (keys, keys), (values, values)
    early_keys, early_values = (halo[0], keys), (halo[1], values)
    gated = (gate_pre, group_gain_f, group_bias_f)
    late_out, late_hat, late_scale = retention(
        late_place, *shared, late_keys, late_values, *gated, rows, *late_rows
    )
    early_out, early_hat, early_scale = retention(
        early_place, *shared, early_keys, early_values, *gated, rows, *early_rows
    )

    if small_mesh:
        out_low_x, out_high_y = stages.run(
            (out_low, by_x), (out_high, by_y), chain=weights_last, late=(gate_pre,)
        )
        out_high_xy, out_low_xy, up_y = stages.run(
            (jnp.stack([out_high, out_high_y]), by_x),
            (jnp.stack([out_low, out_low_x]), by_y),
            (up_four, by_y),
            chain=(),
            joined=False,
        )
        out_held = {
            0: (out_low, out_high),
            1: (out_low_x, out_high_xy[0]),
            2: (out_low_xy[0], out_high_y),
            3: (out_low_xy[1], out_high_xy[1]),
        }
        out_head = jnp.zeros((chips, 2, half_low, width), BF16)
        for d, (low, high) in out_held.items():
            out_head = put(out_head, jnp.stack([low, high])[None], chip ^ d, 0)
        out_head = out_head.reshape(groups * VD, width)
    else:
        out_head = lax.all_gather(out_weight, "seq", axis=0, tiled=True)
        out_head = pick(out_head.reshape(groups, 2, VD, width), core, 1).reshape(groups * VD, width)
    up_held, down_held = {0: up_four}, {0: down_weight}
    if small_mesh:
        up_held[1] = up_y
        down_held[1] = down_y
    else:
        for bit in range(2, devices.bit_length() - 1):
            for held in (up_held, down_held):
                held.update({d | (1 << (bit - 2)): flip(v, 1 << bit) for d, v in list(held.items())})
    up_quarter = jnp.zeros((devices, part, ff_quarter), BF16)
    for e, four in up_held.items():
        for d in range(4):
            up_quarter = put(up_quarter, four[d : d + 1], seq_index ^ (4 * e + d), 0)
    up_quarter = up_quarter.reshape(width, ff_quarter)
    down_quarter = jnp.concatenate(by_difference(down_held, quad), axis=0)

    def with_core(two):
        return jnp.concatenate([two, by_core(two)], axis=0)

    if not small_mesh:
        cotangent_x = by_x(cotangent)
    near_cotangent, far_cotangent = with_core(cotangent), with_core(cotangent_x)

    def exchange(blocks):
        return lax.all_to_all(blocks, "grp", split_axis=0, concat_axis=0, tiled=True)

    def to_tokens(early, late):
        parted = [item.reshape(groups, own_rows, VD) for item in (early, late)]
        came = exchange(jnp.concatenate(parted, axis=1))
        return jnp.concatenate(list(came), axis=1)

    def to_heads(block):
        sent = jnp.stack([block[:, i * VD : (i + 1) * VD] for i in range(groups)])
        came = exchange(sent).reshape(groups, 2, own_rows, VD)
        return jnp.concatenate([came[:, 0].reshape(rows, VD), came[:, 1].reshape(rows, VD)])

    def pair_sum(block, size, kind):
        mine = cut(block, core, size, 0)
        return mine + by_core(cut(block, 1 - core, size, 0).astype(kind)).astype(F32)

    def pair_rows_of(block):
        beside = by_core(block)
        return jnp.concatenate(
            [jnp.where(core == 0, block, beside), jnp.where(core == 0, beside, block)], axis=0
        )

    by_token = to_tokens(early_out, late_out)
    hidden = inputs + pair_sum(dot(by_token, out_head), own_rows, F32)
    normed_two = layer_norm(hidden, gain_two, bias_two).astype(BF16)
    normed_x = by_x(normed_two)
    near_normed, far_normed = with_core(normed_two), with_core(normed_x)
    weights = (up_quarter, down_quarter, up_bias_quarter)
    near_activated, near_grad_pre, near_mixed, near_grad, near_bias = feed(near_normed, near_cotangent, *weights)
    far_activated, far_grad_pre, far_mixed, far_grad, far_bias = feed(far_normed, far_cotangent, *weights)
    up_bias_part = near_bias + far_bias
    grad_out = cotangent.astype(F32)
    down_bias_part = jnp.sum(grad_out, axis=0)

    def plus(mine, came):
        return mine.astype(F32) + came.astype(F32)

    def pair_part(block):
        return plus(block[:own_rows], by_core(block[own_rows:]))

    far_grad = pair_part(far_grad).astype(BF16)
    activated = jnp.concatenate([near_activated, far_activated])
    quad_cotangent = jnp.concatenate([near_cotangent, far_cotangent])
    down_part = dot(activated, quad_cotangent, ((0,), (0,))).astype(BF16).reshape(quads, ff_part, width)
    if small_mesh:
        grad_x, down_y = stages.run((far_grad, by_x), (pick(down_part, 1 - quad), by_y), chain=(), joined=False)
    else:
        grad_x = by_x(far_grad)
    grad_normed_two = plus(pair_part(near_grad), grad_x)
    second_back = jax.vjp(layer_norm, hidden, gain_two, bias_two)[1]
    hidden_part, gain_two_part, bias_two_part = second_back(grad_normed_two)
    grad_hidden = grad_out + hidden_part
    grad_attend = pair_rows_of(grad_hidden.astype(BF16))
    grad_by_token = dot(grad_attend, out_head, ((1,), (1,))).astype(BF16)
    grad_heads = to_heads(grad_by_token)

    quad_normed = jnp.concatenate([near_normed, far_normed])
    quad_grad_pre = jnp.concatenate([near_grad_pre, far_grad_pre])
    up_part = dot(quad_normed, quad_grad_pre, ((0,), (0,))).astype(BF16).reshape(quads, 4, part, ff_quarter)
    out_part = dot(by_token, grad_attend, ((0,), (0,))).astype(BF16)

    def split_chips(parts):
        held, bit = dict(parts), 1
        while bit < chips:
            sent = {d: flip(v.astype(BF16), 2 * bit) for d, v in held.items() if d & bit}
            held = {
                d: v.astype(F32) + sent[d | bit].astype(F32) for d, v in held.items() if not d & bit
            }
            bit *= 2
        return held[0]

    def split_quads(block):
        held, bit = {d: pick(block, quad ^ d) for d in range(quads)}, 1
        while bit < quads:
            sent = {d: flip(v.astype(BF16), 4 * bit) for d, v in held.items() if d & bit}
            held = {
                d: v.astype(F32) + sent[d | bit].astype(F32) for d, v in held.items() if not d & bit
            }
            bit *= 2
        return held[0]

    def up_to_owners(up_four, up_x):
        up_core = by_core(jnp.stack([pick(up_four, quarter ^ 1), up_x[1]]))
        up_blocks = by_difference([pick(up_four, quarter), up_core[0], up_x[0], up_core[1]], quarter)
        return jnp.concatenate(
            [block[:, m * ff_part : (m + 1) * ff_part] for m in range(quads) for block in up_blocks], axis=1
        )

    def up_x_sent(up_four):
        return jnp.stack([pick(up_four, quarter ^ 2), pick(up_four, quarter ^ 3)])

    mixed_sent = pair_part(far_mixed).astype(BF16)
    if small_mesh:
        down_sum = plus(pick(down_part, quad), down_y).astype(BF16)
        out_part = out_part.reshape(chips, 2, half_low, width)
        low, high = ([pick(out_part[:, i], chip ^ d) for d in range(chips)] for i in (0, 1))
        high_x, low_y = stages.run(
            (jnp.stack([high[1], high[3]]), by_x),
            (jnp.stack([low[2], low[3]]), by_y),
            chain=(grad_by_token,),
        )
        low_x, high_y = stages.run(
            (plus(low[1], low_y[1]).astype(BF16), by_x),
            (plus(high[2], high_x[1]).astype(BF16), by_y),
            late=(grad_heads,),
        )
        low_sum = plus(plus(low[0], low_y[0]), low_x).astype(BF16)
        high_sum = plus(plus(high[0], high_x[0]), high_y).astype(BF16)
    else:
        mixed_x = by_x(mixed_sent)
        down_sum = split_quads(down_part).astype(BF16)
        up_four = split_quads(up_part).astype(BF16)
        spread = jnp.zeros((groups, 2, VD, width), BF16)
        spread = put(spread, out_part.reshape(groups, 1, VD, width), core, 1)
        out_sum = lax.psum_scatter(
            spread.reshape(groups * 2 * VD, width), "seq", scatter_dimension=0, tiled=True
        )
        low_sum, high_sum = jnp.split(out_sum, 2)
    half = down_sum.shape[0] // 2
    line = GroupLine(group_index, 6)
    line.add(down_sum[:half], down_sum[half:])
    line.add(low_sum, high_sum)

    early_query, early_gate, later, early_own, early_gain, early_bias = retention_back(
        early_place, *shared, early_keys, early_values, *gated, early_hat, early_scale, grad_heads, rows, *early_rows
    )
    late_query, late_gate, late_own, late_end, late_gain, late_bias = retention_back(
        late_place, *shared, late_keys, late_values, *gated, late_hat, late_scale, grad_heads, rows, *late_rows
    )
    line.step(grad_heads)
    line.step(late_gate)
    group_gain_part, group_bias_part = early_gain + late_gain, early_bias + late_bias
    later = later.astype(BF16)
    if small_mesh:
        out_last = stages.last
        (later,) = stages.run((later, lambda v: hop(v, -2)), chain=(high_x, low_y))
        mixed_x, up_y = stages.run(
            (mixed_sent, by_x), (pick(up_part, 1 - quad), by_y), chain=out_last, late=(late_gate,)
        )
        up_four = plus(pick(up_part, quad), up_y).astype(BF16)
    else:
        later = hop(later, -2)
    chunk_shape = low_sum.shape
    line.add(*(item.reshape(chunk_shape) for item in jnp.split(up_four.reshape(-1), 2)))

    def projection_grads(query, own, gate, begin):
        near = slice(begin, begin + rows)
        turned = (cosine[near], sine[near])
        return jnp.concatenate(
            [
                rotate_back(query, *turned).astype(BF16),
                (rotate_back(own[:, :KD], *turned) * key_scale).astype(BF16),
                own[:, KD:].astype(BF16),
                gate,
            ],
            axis=1,
        )

    early_grads = projection_grads(early_query, early_own + late_own, early_gate, 0)
    line.step(early_grads)
    late_grads = projection_grads(late_query, late_end + later.astype(F32), late_gate, rows)
    line.step(late_grads)
    grads = jnp.concatenate([early_grads, late_grads])

    theirs_part = dot(cut(grads, 1 - core, rows, 0), head_weight, ((1,), (1,))).astype(BF16)
    normed_part = dot(cut(grads, core, rows, 0), head_weight, ((1,), (1,))) + by_core(theirs_part).astype(F32)
    blocks = normed_part.astype(BF16).reshape(groups, own_rows, width)
    own_block = pick(normed_part.reshape(groups, own_rows, width), group_index)
    if small_mesh:
        line.add_blocks(blocks)
        for _ in range(5):
            line.step()
        from_groups = line.last()
    else:
        for _ in range(4):
            line.step()
        block_line = GroupLine(group_index, 0)
        block_line.add_blocks(blocks)
        for _ in range(groups - 1):
            block_line.step()
        from_groups = block_line.last()
    grad_normed = own_block + from_groups
    down_grad = jnp.concatenate([line.total(0), line.total(1)])
    out_grad = jnp.concatenate([line.total(2), line.total(3)])
    up_four = jnp.concatenate([line.total(4).reshape(-1), line.total(5).reshape(-1)]).astype(BF16)
    up_four = up_four.reshape(4, part, ff_quarter)
    head_part = dot(pair_normed, grads, ((0,), (0,))).astype(BF16)
    product_part = jnp.sum(head_part.astype(F32) * head_weight.astype(F32), axis=1)
    bias_one_part = jnp.sum(head_weight.astype(F32) * jnp.sum(grads.astype(F32), axis=0)[None], axis=1)
    gain_one_part = (product_part - bias_one * bias_one_part) / gain_one
    head_part = head_part.reshape(chips, 2, part, columns)
    parts = {d: pick(head_part, chip ^ d) for d in range(chips)}
    if small_mesh:
        high_x, low_y = stages.run(
            (jnp.stack([parts[1][1], parts[3][1]]), by_x),
            (jnp.stack([parts[2][0], parts[3][0]]), by_y),
            late=(normed_part,),
        )
        low_x, high_y = stages.run(
            (plus(parts[1][0], low_y[1]).astype(BF16), by_x),
            (plus(parts[2][1], high_x[1]).astype(BF16), by_y),
        )
        low_sum = plus(plus(parts[0][0], low_y[0]), low_x)
        high_sum = plus(plus(parts[0][1], high_x[0]), high_y)
    else:
        low_sum, high_sum = split_chips(parts)
    up_grad = up_to_owners(up_four, by_x(up_x_sent(up_four))).astype(F32)
    mixed = (hidden + plus(pair_part(near_mixed), mixed_x) + down_bias_full).astype(BF16)
    own_head = jnp.where(core == 0, low_sum, high_sum)
    other_head = by_core(jnp.where(core == 0, high_sum, low_sum).astype(BF16)).astype(F32)
    first_head = jnp.where(core == 0, own_head, other_head)
    second_head = jnp.where(core == 0, other_head, own_head)

    def both_heads(start, size):
        return jnp.concatenate(
            [first_head[:, start : start + size], second_head[:, start : start + size]], axis=1
        )

    query_grad, key_grad = both_heads(0, KD), both_heads(KD, KD)
    value_grad, gate_grad = both_heads(2 * KD, VD), both_heads(2 * KD + VD, VD)

    up_bias_whole = put(jnp.zeros((quads, 4, ff_part), F32), up_bias_part.reshape(quads, 1, ff_part), quarter, 1)
    group_whole = jnp.zeros((groups, 2, 2, VD), F32)
    group_pair = jnp.stack([group_gain_part.reshape(-1), group_bias_part.reshape(-1)])
    group_whole = lax.dynamic_update_slice(group_whole, group_pair[None, None], (group_index, core, 0, 0))
    group_rows = group_whole.reshape(groups, 4, devices, VD // devices).transpose(2, 0, 1, 3)
    pieces = [
        item.reshape(devices, -1)
        for item in (
            gain_one_part,
            bias_one_part,
            gain_two_part,
            bias_two_part,
            down_bias_part,
            up_bias_whole,
            group_rows,
        )
    ]
    sums = small_sum(jnp.concatenate(pieces, axis=1))
    sums = pick(sums, seq_index)
    first_back = jax.vjp(lambda v: layer_norm(v, gain_one, bias_one), inputs)[1]
    tokens_grad = (grad_hidden + first_back(after(grad_normed, sums))[0]).astype(BF16)
    taken, start = [], 0
    for item in pieces:
        taken.append(sums[start : start + item.shape[1]])
        start += item.shape[1]
    first_gain_grad, first_bias_grad, second_gain_grad, second_bias_grad = taken[:4]
    down_bias_grad, up_bias_grad = taken[4:6]
    group_own = pick(taken[6].reshape(groups, 2, 2, VD // devices), group_index)
    group_gain_grad, group_bias_grad = group_own[:, 0].T, group_own[:, 1].T
    return (
        mixed,
        tokens_grad,
        first_gain_grad,
        first_bias_grad,
        query_grad,
        key_grad,
        value_grad,
        gate_grad,
        group_gain_grad,
        group_bias_grad,
        out_grad,
        second_gain_grad,
        second_bias_grad,
        up_grad,
        up_bias_grad,
        down_grad,
        down_bias_grad,
    )


def solution(mesh):
    placed = (
        P(("seq", "grp"), None),
        P("seq"),
        P("seq"),
        P("seq", "grp"),
        P("seq", "grp"),
        P("seq", "grp"),
        P("seq", "grp"),
        P("seq", "grp"),
        P("seq", "grp"),
        P("seq", None),
        P("seq"),
        P("seq"),
        P("seq", None),
        P("seq"),
        P("seq", None),
        P("seq"),
        P(("seq", "grp"), None),
        P(),
        P("grp"),
    )
    return jax.shard_map(
        body,
        mesh=mesh,
        in_specs=placed,
        out_specs=(
            P(("seq", "grp"), None),
            P(("seq", "grp"), None),
            P("seq"),
            P("seq"),
            P("seq", "grp"),
            P("seq", "grp"),
            P("seq", "grp"),
            P("seq", "grp"),
            P("seq", "grp"),
            P("seq", "grp"),
            P("seq", None),
            P("seq"),
            P("seq"),
            P("seq", None),
            P("seq"),
            P("seq", None),
            P("seq"),
        ),
        check_vma=False,
    )
```

```python
import jax
import jax.numpy as jnp
from jax import lax
from jax.experimental import pallas as pl
from jax.experimental.pallas import tpu as pltpu
from jax.sharding import PartitionSpec as P

KD = 256
VD = 512
TILE = 256
VMEM_LIMIT = 48 * 2**20
EPSILON = 1e-05

F32 = jnp.float32
BF16 = jnp.bfloat16


def dot(a, b, dims=((1,), (0,))):
    return lax.dot_general(a, b, (dims, ((), ())), preferred_element_type=F32)


def flip(block, bit):
    devices = lax.axis_size("seq")
    return lax.ppermute(block, "seq", [(i, i ^ bit) for i in range(devices)])


def hop(block, by):
    devices = lax.axis_size("seq")
    return lax.ppermute(block, "seq", [(i, i + by) for i in range(devices) if 0 <= i + by < devices])


def turn(block, by):
    groups = lax.axis_size("grp")
    return lax.ppermute(block, "grp", [(i, (i + by) % groups) for i in range(groups)])


def pick(array, index, axis=0):
    return lax.dynamic_index_in_dim(array, index, axis, keepdims=False)


def cut(array, index, size, axis):
    return lax.dynamic_slice_in_dim(array, index * size, size, axis)


def put(array, block, index, axis):
    return lax.dynamic_update_slice_in_dim(array, block, index * block.shape[axis], axis)


def after(block, *others):
    return lax.optimization_barrier((block, *others))[0]


class Stages:
    def __init__(self):
        self.last = ()

    def run(self, *sends, late=(), chain=None, joined=True):
        first = tuple(self.last if chain is None else chain) + tuple(late)
        blocks = lax.optimization_barrier(tuple(b for b, _ in sends) + first)
        came = tuple(move(block) for block, (_, move) in zip(blocks, sends))
        came = lax.optimization_barrier(came) if joined and len(came) > 1 else came
        self.last = came
        return came


def by_core(block):
    return flip(block, 1)


def by_x(block):
    return flip(block, 2)


def by_y(block):
    return flip(block, 4)


def choose(index, options):
    result = options[0]
    for i, option in enumerate(options[1:], 1):
        result = jnp.where(index == i, option, result)
    return result


def by_difference(blocks, index):
    count = len(blocks)
    return [choose(index ^ i, [blocks[d] for d in range(count)]) for i in range(count)]


class GroupLine:
    def __init__(self, group_index, count):
        self.groups = lax.axis_size("grp")
        self.index, self.count = group_index, count
        self.pieces = {}
        self.came = {"up": [], "down": []}

    def add(self, *pieces):
        for piece in lax.optimization_barrier(pieces):
            self.pieces[len(self.pieces)] = (piece, piece)

    def add_blocks(self, blocks):
        blocks = lax.optimization_barrier(tuple(blocks))
        for i in range(self.groups - 1):
            self.pieces[self.count + i] = (blocks[self.groups - 1 - i], blocks[i])

    def step(self, *late):
        step, groups = len(self.came["up"]), self.groups
        sends = []
        for way, place in (("up", self.index), ("down", groups - 1 - self.index)):
            side = 0 if way == "up" else 1
            pairs, options = [], []
            for p in range(groups - 1):
                item = step - p
                ahead = item - self.count
                live = item in self.pieces and (ahead < 0 or p + 1 <= groups - 1 - ahead)
                if live:
                    pairs.append((p, p + 1) if side == 0 else (groups - 1 - p, groups - 2 - p))
                options.append(self.pieces[item][side] if live else None)
            known = next(option for option in options if option is not None)
            sent = choose(place, [known if option is None else option for option in options])
            if step:
                sent = (sent.astype(F32) + self.came[way][-1].astype(F32)).astype(BF16)
            sends.append((sent, pairs))
        blocks = lax.optimization_barrier(tuple(sent for sent, _ in sends) + late)
        for way, block, (_, pairs) in zip(("up", "down"), blocks, sends):
            self.came[way].append(lax.ppermute(block, "grp", pairs))

    def total(self, item):
        groups = self.groups
        piece = self.pieces[item][0]
        zero = jnp.zeros_like(piece)
        below = choose(self.index, [zero] + self.came["up"][item : item + groups - 1])
        above = choose(groups - 1 - self.index, [zero] + self.came["down"][item : item + groups - 1])
        return piece.astype(F32) + below.astype(F32) + above.astype(F32)

    def last(self):
        step = self.count + self.groups - 2
        return self.came["up"][step].astype(F32) + self.came["down"][step].astype(F32)


def small_sum(block):
    bit = lax.axis_size("seq") // 2
    while bit:
        mine = lax.axis_index("seq") // bit % 2
        block = cut(block, mine, bit, 0) + flip(cut(block, 1 - mine, bit, 0), bit)
        bit //= 2
    groups, bit = lax.axis_size("grp"), 1
    while bit < groups:
        block = block + lax.ppermute(block, "grp", [(i, i ^ bit) for i in range(groups)])
        bit *= 2
    return block


def layer_norm(values, gain, bias):
    center = values - jnp.mean(values, axis=-1, keepdims=True)
    spread = jnp.mean(center * center, axis=-1, keepdims=True)
    return center * lax.rsqrt(spread + EPSILON) * gain + bias


def document_table(doc_lengths, positions):
    ends = jnp.cumsum(doc_lengths, dtype=jnp.int32)
    after = (positions[:, None] >= ends[None, :]).astype(jnp.int32)
    documents = jnp.sum(after, axis=1, dtype=jnp.int32)
    starts = jnp.sum(after * doc_lengths[None, :], axis=1, dtype=jnp.int32)
    return (documents, positions - starts)


def rotary_table(places, width):
    half = width // 2
    freqs = 10000.0 ** (-jnp.arange(half, dtype=F32) / (half - 1))
    angles = places.astype(F32)[:, None] * freqs[None, :]
    return jnp.cos(angles), jnp.sin(angles)


def rotate(values, cosine, sine):
    half = values.shape[-1] // 2
    low, high = values[:, :half], values[:, half:]
    return jnp.concatenate([low * cosine - high * sine, high * cosine + low * sine], axis=1)


def rotate_back(grads, cosine, sine):
    return rotate(grads, cosine, -sine)


def tile_bounds(starts_ref, window, first, rows, axis):
    shape = (rows, 1) if axis == 0 else (1, rows)
    position = first + lax.broadcasted_iota(jnp.int32, shape, axis)
    earliest = jnp.maximum(position - window + 1, 0)
    for d in range(starts_ref.shape[0]):
        begin = starts_ref[d]
        earliest = jnp.where(position >= begin, jnp.maximum(earliest, begin), earliest)
    return position, earliest


def retention_kernel(
    place_ref,
    starts_ref,
    decay_ref,
    query_ref,
    key_low_ref,
    key_high_ref,
    value_low_ref,
    value_high_ref,
    gate_ref,
    gain_ref,
    bias_ref,
    out_ref,
    hat_ref,
    scale_ref,
):
    half = key_low_ref.shape[0]
    log_decay = decay_ref[0]
    for tile in range(query_ref.shape[0] // TILE):
        begin = tile * TILE
        first = place_ref[0] + begin
        rows = slice(begin, begin + TILE)
        position, earliest = tile_bounds(starts_ref, place_ref[1], first, TILE, 0)
        row_decay = jnp.exp((position - first).astype(F32) * log_decay)
        total = jnp.zeros((TILE, VD), F32)
        for keys, values, low, high, offset in (
            (key_low_ref, value_low_ref, begin, half, begin - half),
            (key_high_ref, value_high_ref, 0, begin + TILE, begin * 0),
        ):
            count = high - low
            ahead = (low - begin) - (half if keys is key_low_ref else 0)
            column = first + ahead + lax.broadcasted_iota(jnp.int32, (1, count), 1)
            column_decay = jnp.exp((first - column).astype(F32) * log_decay)
            scores = dot(query_ref[rows, :], keys[low:high, :], ((1,), (1,)))
            inside = (column <= position) & (column >= earliest)
            weights = jnp.where(inside, scores * (row_decay * column_decay), 0.0).astype(BF16)
            total = total + dot(weights, values[low:high, :])
        center = total - jnp.mean(total, axis=1, keepdims=True)
        scale = lax.rsqrt(jnp.mean(center * center, axis=1, keepdims=True) + EPSILON)
        hat = center * scale
        gate = gate_ref[rows, :].astype(F32)
        silu = gate / (1.0 + jnp.exp(-gate))
        out_ref[rows, :] = (silu * (hat * gain_ref[...] + bias_ref[...])).astype(BF16)
        hat_ref[rows, :] = hat.astype(BF16)
        scale_ref[rows, :] = jnp.broadcast_to(scale, (TILE, 128))


def retention_back_kernel(
    place_ref,
    starts_ref,
    decay_ref,
    query_ref,
    key_low_ref,
    key_high_ref,
    value_low_ref,
    value_high_ref,
    gate_ref,
    gain_ref,
    bias_ref,
    hat_ref,
    scale_ref,
    grad_ref,
    query_grad_ref,
    gate_grad_ref,
    low_grad_ref,
    high_grad_ref,
    gain_grad_ref,
    bias_grad_ref,
):
    half = key_low_ref.shape[0]
    log_decay = decay_ref[0]
    gain, bias = gain_ref[...], bias_ref[...]
    gain_grad = jnp.zeros((1, VD), F32)
    bias_grad = jnp.zeros((1, VD), F32)
    low_grad_ref[...] = jnp.zeros_like(low_grad_ref)
    high_grad_ref[...] = jnp.zeros_like(high_grad_ref)
    for tile in range(query_ref.shape[0] // TILE):
        begin = tile * TILE
        first = place_ref[0] + begin
        rows = slice(begin, begin + TILE)
        hat = hat_ref[rows, :].astype(F32)
        grad = grad_ref[rows, :].astype(F32)
        gate = gate_ref[rows, :].astype(F32)
        sigmoid = 1.0 / (1.0 + jnp.exp(-gate))
        silu = gate * sigmoid
        grouped_grad = grad * silu
        gate_grad = grad * (hat * gain + bias) * (sigmoid + silu * (1.0 - sigmoid))
        gate_grad_ref[rows, :] = gate_grad.astype(BF16)
        gain_grad = gain_grad + jnp.sum(grouped_grad * hat, axis=0, keepdims=True)
        bias_grad = bias_grad + jnp.sum(grouped_grad, axis=0, keepdims=True)
        inner = grouped_grad * gain
        mean = jnp.mean(inner, axis=1, keepdims=True)
        along = jnp.mean(inner * hat, axis=1, keepdims=True)
        kept_grad = ((inner - mean - hat * along) * scale_ref[rows, :1]).astype(BF16)
        query = query_ref[rows, :]
        position, earliest = tile_bounds(starts_ref, place_ref[1], first, TILE, 1)
        row_decay = jnp.exp((position - first).astype(F32) * log_decay)
        query_grad = jnp.zeros((TILE, KD), F32)
        for keys, values, sums, low, high in (
            (key_low_ref, value_low_ref, low_grad_ref, begin, half),
            (key_high_ref, value_high_ref, high_grad_ref, 0, begin + TILE),
        ):
            count = high - low
            ahead = (low - begin) - (half if keys is key_low_ref else 0)
            column = first + ahead + lax.broadcasted_iota(jnp.int32, (count, 1), 0)
            column_decay = jnp.exp((first - column).astype(F32) * log_decay)
            inside = (column <= position) & (column >= earliest)
            mask = jnp.where(inside, row_decay * column_decay, 0.0)
            key, value = keys[low:high, :], values[low:high, :]
            weights = (dot(key, query, ((1,), (1,))) * mask).astype(BF16)
            scores = (dot(value, kept_grad, ((1,), (1,))) * mask).astype(BF16)
            sums[low:high, KD:] += dot(weights, kept_grad)
            sums[low:high, :KD] += dot(scores, query)
            query_grad = query_grad + dot(scores, key, ((0,), (0,)))
        query_grad_ref[rows, :] = query_grad
    gain_grad_ref[...] = gain_grad
    bias_grad_ref[...] = bias_grad


def whole_spec(*shape):
    return pl.BlockSpec(shape, lambda _: (0,) * len(shape))


def retention_specs(rows, low, high):
    def part(width, index):
        return pl.BlockSpec((rows, width), lambda _: (index, 0))

    smem = pl.BlockSpec(memory_space=pltpu.SMEM)
    return [smem] * 3 + [
        part(KD, high[1]),
        part(KD, low),
        part(KD, high[0]),
        part(VD, low),
        part(VD, high[0]),
        part(VD, high[1]),
        whole_spec(1, VD),
        whole_spec(1, VD),
    ]


def retention(place, starts, decay, queries, keys, values, gate, gain, bias, rows, low, high):
    cost = pl.CostEstimate(flops=rows * 1280 * 192, bytes_accessed=rows * 1024, transcendentals=0)
    return pl.pallas_call(
        retention_kernel,
        out_shape=(
            jax.ShapeDtypeStruct((rows, VD), BF16),
            jax.ShapeDtypeStruct((rows, VD), BF16),
            jax.ShapeDtypeStruct((rows, 128), F32),
        ),
        grid=(1,),
        in_specs=retention_specs(rows, low, high),
        out_specs=(whole_spec(rows, VD), whole_spec(rows, VD), whole_spec(rows, 128)),
        compiler_params=pltpu.CompilerParams(vmem_limit_bytes=VMEM_LIMIT),
        cost_estimate=cost,
    )(place, starts, decay, queries, keys[0], keys[1], values[0], values[1], gate, gain, bias)


def retention_back(
    place, starts, decay, queries, keys, values, gate, gain, bias, hat, scale, grad, rows, low, high
):
    cost = pl.CostEstimate(flops=rows * 1280 * 448, bytes_accessed=rows * 2048, transcendentals=0)
    part = pl.BlockSpec((rows, VD), lambda _: (high[1], 0))
    return pl.pallas_call(
        retention_back_kernel,
        out_shape=(
            jax.ShapeDtypeStruct((rows, KD), F32),
            jax.ShapeDtypeStruct((rows, VD), BF16),
            jax.ShapeDtypeStruct((rows, KD + VD), F32),
            jax.ShapeDtypeStruct((rows, KD + VD), F32),
            jax.ShapeDtypeStruct((1, VD), F32),
            jax.ShapeDtypeStruct((1, VD), F32),
        ),
        grid=(1,),
        in_specs=retention_specs(rows, low, high)
        + [whole_spec(rows, VD), whole_spec(rows, 128), part],
        out_specs=(
            whole_spec(rows, KD),
            whole_spec(rows, VD),
            whole_spec(rows, KD + VD),
            whole_spec(rows, KD + VD),
            whole_spec(1, VD),
            whole_spec(1, VD),
        ),
        compiler_params=pltpu.CompilerParams(vmem_limit_bytes=VMEM_LIMIT),
        cost_estimate=cost,
    )(place, starts, decay, queries, keys[0], keys[1], values[0], values[1], gate, gain, bias, hat, scale, grad)


def feed_kernel(
    normed_ref,
    cotangent_ref,
    up_ref,
    down_ref,
    bias_ref,
    activated_ref,
    grad_pre_ref,
    mixed_ref,
    grad_ref,
    bias_grad_ref,
):
    up, down = up_ref[...], down_ref[...]
    pre = dot(normed_ref[...], up) + bias_ref[...]
    grad_act = dot(cotangent_ref[...], down, ((1,), (1,)))
    share = 0.5 + 0.5 * lax.erf(pre * 0.7071067811865476)
    bell = jnp.exp(-0.5 * pre * pre) * 0.3989422804014327
    activated = (pre * share).astype(BF16)
    grad_pre = (grad_act * (share + pre * bell)).astype(BF16)
    activated_ref[...] = activated
    grad_pre_ref[...] = grad_pre
    mixed_ref[...] = dot(activated, down).astype(BF16)
    grad_ref[...] = dot(grad_pre, up, ((1,), (1,))).astype(BF16)

    @pl.when(pl.program_id(0) == 0)
    def _():
        bias_grad_ref[...] = jnp.zeros_like(bias_grad_ref)

    bias_grad_ref[...] += jnp.sum(grad_pre.astype(F32), axis=0, keepdims=True)


def feed(normed, cotangent, up, down, bias):
    rows, width = normed.shape
    hidden = up.shape[1]

    def tiled(columns):
        return pl.BlockSpec((TILE, columns), lambda i: (i, 0))

    cost = pl.CostEstimate(
        flops=rows * width * hidden, bytes_accessed=rows * width, transcendentals=0
    )
    return pl.pallas_call(
        feed_kernel,
        out_shape=(
            jax.ShapeDtypeStruct((rows, hidden), BF16),
            jax.ShapeDtypeStruct((rows, hidden), BF16),
            jax.ShapeDtypeStruct((rows, width), BF16),
            jax.ShapeDtypeStruct((rows, width), BF16),
            jax.ShapeDtypeStruct((1, hidden), F32),
        ),
        grid=(rows // TILE,),
        in_specs=[
            tiled(width),
            tiled(width),
            whole_spec(*up.shape),
            whole_spec(*down.shape),
            whole_spec(1, hidden),
        ],
        out_specs=(tiled(hidden), tiled(hidden), tiled(width), tiled(width), whole_spec(1, hidden)),
        compiler_params=pltpu.CompilerParams(vmem_limit_bytes=VMEM_LIMIT),
        cost_estimate=cost,
    )(normed, cotangent, up, down, bias)
def body(
    tokens,
    first_gain,
    first_bias,
    query_weight,
    key_weight,
    value_weight,
    gate_weight,
    group_gain,
    group_bias,
    out_weight,
    second_gain,
    second_bias,
    up_weight,
    up_bias,
    down_weight,
    down_bias,
    cotangent,
    doc_lengths,
    windows,
):
    devices, groups = lax.axis_size("seq"), lax.axis_size("grp")
    seq_index, group_index = lax.axis_index("seq"), lax.axis_index("grp")
    chips, quads = devices // 2, devices // 4
    core, chip = seq_index % 2, seq_index // 2
    quarter, quad = seq_index % 4, seq_index // 4
    own_rows, width = tokens.shape
    part = width // devices
    rows = own_rows * groups
    pair_rows = 2 * rows
    ff = up_weight.shape[1]
    ff_part, ff_quarter = ff // devices, ff // 4
    small_mesh = devices == 8
    stages = Stages()

    def head_columns(j):
        return jnp.concatenate(
            [
                cut(query_weight, j, KD, 1),
                cut(key_weight, j, KD, 1),
                cut(value_weight, j, VD, 1),
                cut(gate_weight, j, VD, 1),
            ],
            axis=1,
        )

    mine = head_columns(core)
    theirs = by_core(head_columns(1 - core))
    low_rows = jnp.where(core == 0, mine, theirs)
    high_rows = jnp.where(core == 0, theirs, mine)
    columns = mine.shape[1]

    small = [first_gain, first_bias, second_gain, second_bias, down_bias, up_bias]
    small += [group_gain.T.reshape(-1), group_bias.T.reshape(-1)]
    sizes = [item.shape[0] for item in small]
    packed = lax.all_gather(after(jnp.concatenate(small)[None], low_rows, high_rows), "seq", axis=0, tiled=True).astype(F32)
    whole, start = [], 0
    for size in sizes:
        whole.append(packed[:, start : start + size])
        start += size
    gain_one, bias_one, gain_two, bias_two, down_bias_full, up_bias_full = (
        item.reshape(-1) for item in whole[:6]
    )
    group_gain_f, group_bias_f = (
        pick(item.reshape(devices, 2, -1), core, 1).reshape(1, VD) for item in whole[6:]
    )
    up_bias_quarter = pick(up_bias_full.reshape(quads, 4, ff_part), quarter, 1).reshape(1, ff_quarter)

    inputs = tokens.astype(F32)
    normed = layer_norm(inputs, gain_one, bias_one).astype(BF16)
    gathered = lax.all_gather(normed, "grp", axis=0, tiled=True)

    base = chip * pair_rows
    positions = base + jnp.arange(pair_rows, dtype=jnp.int32)
    places = document_table(doc_lengths, positions)[1]
    doc_starts = jnp.cumsum(doc_lengths, dtype=jnp.int32) - doc_lengths
    cosine, sine = rotary_table(places, KD)
    def join_chips(low, high):
        held = {0: jnp.stack([low, high])}
        for bit in range(1, devices.bit_length() - 1):
            held.update({d | (1 << (bit - 1)): flip(v, 1 << bit) for d, v in list(held.items())})
        return {d: (v[0], v[1]) for d, v in held.items()}

    def quarter_columns(q):
        return [
            lax.dynamic_slice_in_dim(up_weight, (q + 4 * m) * ff_part, ff_part, 1) for m in range(quads)
        ]

    up_sent = jnp.concatenate(quarter_columns(quarter ^ 2) + quarter_columns(quarter ^ 3), axis=1)
    if small_mesh:
        half_low = VD // 2
        out_low, out_high = out_weight[:half_low], out_weight[half_low:]
        low_x, high_y = stages.run((low_rows, by_x), (high_rows, by_y))
        high_xy, low_xy = stages.run(
            (jnp.stack([high_rows, high_y]), by_x), (jnp.stack([low_rows, low_x]), by_y)
        )
        head_held = {
            0: (low_rows, high_rows),
            1: (low_x, high_xy[0]),
            2: (low_xy[0], high_y),
            3: (low_xy[1], high_xy[1]),
        }
        two_x, down_y = stages.run((jnp.stack([up_sent, cotangent]), by_x), (down_weight, by_y))
        up_x, cotangent_x = two_x[0], two_x[1]
        gathered = after(gathered, high_xy, low_xy, cosine, sine)
    else:
        head_held = join_chips(low_rows, high_rows)
        up_x = by_x(up_sent)
    head_weight = jnp.zeros((chips, 2, part, columns), BF16)
    for d, (low, high) in head_held.items():
        head_weight = put(head_weight, jnp.stack([low, high])[None], chip ^ d, 0)
    head_weight = head_weight.reshape(width, columns)

    up_core = by_core(
        jnp.stack([jnp.concatenate(quarter_columns(quarter ^ 1), axis=1), up_x[:, ff_quarter:]])
    )
    up_own = jnp.concatenate(quarter_columns(quarter), axis=1)
    up_four = jnp.stack([up_own, up_core[0], up_x[:, :ff_quarter], up_core[1]])

    beside = by_core(gathered)
    pair_normed = jnp.concatenate(
        [jnp.where(core == 0, gathered, beside), jnp.where(core == 0, beside, gathered)], axis=0
    )

    key_scale = KD ** (-0.5)
    key_pre = dot(pair_normed, head_weight[:, KD : 2 * KD])
    keys = (rotate(key_pre, cosine, sine) * key_scale).astype(BF16)
    values = dot(pair_normed, head_weight[:, 2 * KD : 2 * KD + VD]).astype(BF16)
    halo = jnp.concatenate([keys[rows:], values[rows:]], axis=1)
    if small_mesh:
        weights_last = stages.last
        (halo,) = stages.run((halo, lambda v: hop(v, 2)), chain=(high_xy, low_xy))
    else:
        halo = hop(halo, 2)
    query_pre = dot(pair_normed, head_weight[:, :KD])
    gate_pre = dot(pair_normed, head_weight[:, 2 * KD + VD :]).astype(BF16)
    queries = rotate(query_pre, cosine, sine).astype(BF16)
    halo = (halo[:, :KD], halo[:, KD:])
    head_index = (group_index * 2 + core).astype(F32)
    log_decay = jnp.log1p(-jnp.exp2(-5.0 - head_index)).reshape(1)
    window = windows[0]

    shared = (doc_starts, log_decay, queries)
    late_rows, early_rows = (0, (1, 1)), (0, (0, 0))
    late_place = jnp.stack([base + rows, window])
    early_place = jnp.stack([base, window])
    late_keys, late_values = (keys, keys), (values, values)
    early_keys, early_values = (halo[0], keys), (halo[1], values)
    gated = (gate_pre, group_gain_f, group_bias_f)
    late_out, late_hat, late_scale = retention(
        late_place, *shared, late_keys, late_values, *gated, rows, *late_rows
    )
    early_out, early_hat, early_scale = retention(
        early_place, *shared, early_keys, early_values, *gated, rows, *early_rows
    )

    if small_mesh:
        out_low_x, out_high_y = stages.run(
            (out_low, by_x), (out_high, by_y), chain=weights_last, late=(gate_pre,)
        )
        out_high_xy, out_low_xy, up_y = stages.run(
            (jnp.stack([out_high, out_high_y]), by_x),
            (jnp.stack([out_low, out_low_x]), by_y),
            (up_four, by_y),
            chain=(),
            joined=False,
        )
        out_held = {
            0: (out_low, out_high),
            1: (out_low_x, out_high_xy[0]),
            2: (out_low_xy[0], out_high_y),
            3: (out_low_xy[1], out_high_xy[1]),
        }
        out_head = jnp.zeros((chips, 2, half_low, width), BF16)
        for d, (low, high) in out_held.items():
            out_head = put(out_head, jnp.stack([low, high])[None], chip ^ d, 0)
        out_head = out_head.reshape(groups * VD, width)
    else:
        out_head = lax.all_gather(out_weight, "seq", axis=0, tiled=True)
        out_head = pick(out_head.reshape(groups, 2, VD, width), core, 1).reshape(groups * VD, width)
    up_held, down_held = {0: up_four}, {0: down_weight}
    if small_mesh:
        up_held[1] = up_y
        down_held[1] = down_y
    else:
        for bit in range(2, devices.bit_length() - 1):
            for held in (up_held, down_held):
                held.update({d | (1 << (bit - 2)): flip(v, 1 << bit) for d, v in list(held.items())})
    up_quarter = jnp.zeros((devices, part, ff_quarter), BF16)
    for e, four in up_held.items():
        for d in range(4):
            up_quarter = put(up_quarter, four[d : d + 1], seq_index ^ (4 * e + d), 0)
    up_quarter = up_quarter.reshape(width, ff_quarter)
    down_quarter = jnp.concatenate(by_difference(down_held, quad), axis=0)

    def with_core(two):
        return jnp.concatenate([two, by_core(two)], axis=0)

    if not small_mesh:
        cotangent_x = by_x(cotangent)
    near_cotangent, far_cotangent = with_core(cotangent), with_core(cotangent_x)

    def exchange(blocks):
        return lax.all_to_all(blocks, "grp", split_axis=0, concat_axis=0, tiled=True)

    def to_tokens(early, late):
        parted = [item.reshape(groups, own_rows, VD) for item in (early, late)]
        came = exchange(jnp.concatenate(parted, axis=1))
        return jnp.concatenate(list(came), axis=1)

    def to_heads(block):
        sent = jnp.stack([block[:, i * VD : (i + 1) * VD] for i in range(groups)])
        came = exchange(sent).reshape(groups, 2, own_rows, VD)
        return jnp.concatenate([came[:, 0].reshape(rows, VD), came[:, 1].reshape(rows, VD)])

    def pair_sum(block, size, kind):
        mine = cut(block, core, size, 0)
        return mine + by_core(cut(block, 1 - core, size, 0).astype(kind)).astype(F32)

    def pair_rows_of(block):
        beside = by_core(block)
        return jnp.concatenate(
            [jnp.where(core == 0, block, beside), jnp.where(core == 0, beside, block)], axis=0
        )

    by_token = to_tokens(early_out, late_out)
    hidden = inputs + pair_sum(dot(by_token, out_head), own_rows, F32)
    normed_two = layer_norm(hidden, gain_two, bias_two).astype(BF16)
    normed_x = by_x(normed_two)
    near_normed, far_normed = with_core(normed_two), with_core(normed_x)
    weights = (up_quarter, down_quarter, up_bias_quarter)
    near_activated, near_grad_pre, near_mixed, near_grad, near_bias = feed(near_normed, near_cotangent, *weights)
    far_activated, far_grad_pre, far_mixed, far_grad, far_bias = feed(far_normed, far_cotangent, *weights)
    up_bias_part = near_bias + far_bias
    grad_out = cotangent.astype(F32)
    down_bias_part = jnp.sum(grad_out, axis=0)

    def plus(mine, came):
        return mine.astype(F32) + came.astype(F32)

    def pair_part(block):
        return plus(block[:own_rows], by_core(block[own_rows:]))

    far_grad = pair_part(far_grad).astype(BF16)
    activated = jnp.concatenate([near_activated, far_activated])
    quad_cotangent = jnp.concatenate([near_cotangent, far_cotangent])
    down_part = dot(activated, quad_cotangent, ((0,), (0,))).astype(BF16).reshape(quads, ff_part, width)
    if small_mesh:
        grad_x, down_y = stages.run((far_grad, by_x), (pick(down_part, 1 - quad), by_y), chain=(), joined=False)
    else:
        grad_x = by_x(far_grad)
    grad_normed_two = plus(pair_part(near_grad), grad_x)
    second_back = jax.vjp(layer_norm, hidden, gain_two, bias_two)[1]
    hidden_part, gain_two_part, bias_two_part = second_back(grad_normed_two)
    grad_hidden = grad_out + hidden_part
    grad_attend = pair_rows_of(grad_hidden.astype(BF16))
    grad_by_token = dot(grad_attend, out_head, ((1,), (1,))).astype(BF16)
    grad_heads = to_heads(grad_by_token)

    quad_normed = jnp.concatenate([near_normed, far_normed])
    quad_grad_pre = jnp.concatenate([near_grad_pre, far_grad_pre])
    up_part = dot(quad_normed, quad_grad_pre, ((0,), (0,))).astype(BF16).reshape(quads, 4, part, ff_quarter)
    out_part = dot(by_token, grad_attend, ((0,), (0,))).astype(BF16)

    def split_chips(parts):
        held, bit = dict(parts), 1
        while bit < chips:
            sent = {d: flip(v.astype(BF16), 2 * bit) for d, v in held.items() if d & bit}
            held = {
                d: v.astype(F32) + sent[d | bit].astype(F32) for d, v in held.items() if not d & bit
            }
            bit *= 2
        return held[0]

    def split_quads(block):
        held, bit = {d: pick(block, quad ^ d) for d in range(quads)}, 1
        while bit < quads:
            sent = {d: flip(v.astype(BF16), 4 * bit) for d, v in held.items() if d & bit}
            held = {
                d: v.astype(F32) + sent[d | bit].astype(F32) for d, v in held.items() if not d & bit
            }
            bit *= 2
        return held[0]

    def up_to_owners(up_four, up_x):
        up_core = by_core(jnp.stack([pick(up_four, quarter ^ 1), up_x[1]]))
        up_blocks = by_difference([pick(up_four, quarter), up_core[0], up_x[0], up_core[1]], quarter)
        return jnp.concatenate(
            [block[:, m * ff_part : (m + 1) * ff_part] for m in range(quads) for block in up_blocks], axis=1
        )

    def up_x_sent(up_four):
        return jnp.stack([pick(up_four, quarter ^ 2), pick(up_four, quarter ^ 3)])

    mixed_sent = pair_part(far_mixed).astype(BF16)
    if small_mesh:
        down_sum = plus(pick(down_part, quad), down_y).astype(BF16)
        out_part = out_part.reshape(chips, 2, half_low, width)
        low, high = ([pick(out_part[:, i], chip ^ d) for d in range(chips)] for i in (0, 1))
        high_x, low_y = stages.run(
            (jnp.stack([high[1], high[3]]), by_x),
            (jnp.stack([low[2], low[3]]), by_y),
            chain=(grad_by_token,),
        )
        low_x, high_y = stages.run(
            (plus(low[1], low_y[1]).astype(BF16), by_x),
            (plus(high[2], high_x[1]).astype(BF16), by_y),
            late=(grad_heads,),
        )
        low_sum = plus(plus(low[0], low_y[0]), low_x).astype(BF16)
        high_sum = plus(plus(high[0], high_x[0]), high_y).astype(BF16)
    else:
        mixed_x = by_x(mixed_sent)
        down_sum = split_quads(down_part).astype(BF16)
        up_four = split_quads(up_part).astype(BF16)
        spread = jnp.zeros((groups, 2, VD, width), BF16)
        spread = put(spread, out_part.reshape(groups, 1, VD, width), core, 1)
        out_sum = lax.psum_scatter(
            spread.reshape(groups * 2 * VD, width), "seq", scatter_dimension=0, tiled=True
        )
        low_sum, high_sum = jnp.split(out_sum, 2)
    half = down_sum.shape[0] // 2
    line = GroupLine(group_index, 6)
    line.add(down_sum[:half], down_sum[half:])
    line.add(low_sum, high_sum)

    early_query, early_gate, later, early_own, early_gain, early_bias = retention_back(
        early_place, *shared, early_keys, early_values, *gated, early_hat, early_scale, grad_heads, rows, *early_rows
    )
    late_query, late_gate, late_own, late_end, late_gain, late_bias = retention_back(
        late_place, *shared, late_keys, late_values, *gated, late_hat, late_scale, grad_heads, rows, *late_rows
    )
    line.step(grad_heads)
    line.step(late_gate)
    group_gain_part, group_bias_part = early_gain + late_gain, early_bias + late_bias
    later = later.astype(BF16)
    if small_mesh:
        out_last = stages.last
        (later,) = stages.run((later, lambda v: hop(v, -2)), chain=(high_x, low_y))
        mixed_x, up_y = stages.run(
            (mixed_sent, by_x), (pick(up_part, 1 - quad), by_y), chain=out_last, late=(late_gate,)
        )
        up_four = plus(pick(up_part, quad), up_y).astype(BF16)
    else:
        later = hop(later, -2)
    chunk_shape = low_sum.shape
    line.add(*(item.reshape(chunk_shape) for item in jnp.split(up_four.reshape(-1), 2)))

    def projection_grads(query, own, gate, begin):
        near = slice(begin, begin + rows)
        turned = (cosine[near], sine[near])
        return jnp.concatenate(
            [
                rotate_back(query, *turned).astype(BF16),
                (rotate_back(own[:, :KD], *turned) * key_scale).astype(BF16),
                own[:, KD:].astype(BF16),
                gate,
            ],
            axis=1,
        )

    early_grads = projection_grads(early_query, early_own + late_own, early_gate, 0)
    line.step(early_grads)
    late_grads = projection_grads(late_query, late_end + later.astype(F32), late_gate, rows)
    line.step(late_grads)
    grads = jnp.concatenate([early_grads, late_grads])

    theirs_part = dot(cut(grads, 1 - core, rows, 0), head_weight, ((1,), (1,))).astype(BF16)
    normed_part = dot(cut(grads, core, rows, 0), head_weight, ((1,), (1,))) + by_core(theirs_part).astype(F32)
    blocks = normed_part.astype(BF16).reshape(groups, own_rows, width)
    own_block = pick(normed_part.reshape(groups, own_rows, width), group_index)
    if small_mesh:
        line.add_blocks(blocks)
        for _ in range(5):
            line.step()
        from_groups = line.last()
    else:
        for _ in range(4):
            line.step()
        block_line = GroupLine(group_index, 0)
        block_line.add_blocks(blocks)
        for _ in range(groups - 1):
            block_line.step()
        from_groups = block_line.last()
    grad_normed = own_block + from_groups
    down_grad = jnp.concatenate([line.total(0), line.total(1)])
    out_grad = jnp.concatenate([line.total(2), line.total(3)])
    up_four = jnp.concatenate([line.total(4).reshape(-1), line.total(5).reshape(-1)]).astype(BF16)
    up_four = up_four.reshape(4, part, ff_quarter)
    head_part = dot(pair_normed, grads, ((0,), (0,))).astype(BF16)
    product_part = jnp.sum(head_part.astype(F32) * head_weight.astype(F32), axis=1)
    bias_one_part = jnp.sum(head_weight.astype(F32) * jnp.sum(grads.astype(F32), axis=0)[None], axis=1)
    gain_one_part = (product_part - bias_one * bias_one_part) / gain_one
    head_part = head_part.reshape(chips, 2, part, columns)
    parts = {d: pick(head_part, chip ^ d) for d in range(chips)}
    if small_mesh:
        high_x, low_y = stages.run(
            (jnp.stack([parts[1][1], parts[3][1]]), by_x),
            (jnp.stack([parts[2][0], parts[3][0]]), by_y),
            late=(normed_part,),
        )
        low_x, high_y = stages.run(
            (plus(parts[1][0], low_y[1]).astype(BF16), by_x),
            (plus(parts[2][1], high_x[1]).astype(BF16), by_y),
        )
        low_sum = plus(plus(parts[0][0], low_y[0]), low_x)
        high_sum = plus(plus(parts[0][1], high_x[0]), high_y)
    else:
        low_sum, high_sum = split_chips(parts)
    up_grad = up_to_owners(up_four, by_x(up_x_sent(up_four))).astype(F32)
    mixed = (hidden + plus(pair_part(near_mixed), mixed_x) + down_bias_full).astype(BF16)
    own_head = jnp.where(core == 0, low_sum, high_sum)
    other_head = by_core(jnp.where(core == 0, high_sum, low_sum).astype(BF16)).astype(F32)
    first_head = jnp.where(core == 0, own_head, other_head)
    second_head = jnp.where(core == 0, other_head, own_head)

    def both_heads(start, size):
        return jnp.concatenate(
            [first_head[:, start : start + size], second_head[:, start : start + size]], axis=1
        )

    query_grad, key_grad = both_heads(0, KD), both_heads(KD, KD)
    value_grad, gate_grad = both_heads(2 * KD, VD), both_heads(2 * KD + VD, VD)

    up_bias_whole = put(jnp.zeros((quads, 4, ff_part), F32), up_bias_part.reshape(quads, 1, ff_part), quarter, 1)
    group_whole = jnp.zeros((groups, 2, 2, VD), F32)
    group_pair = jnp.stack([group_gain_part.reshape(-1), group_bias_part.reshape(-1)])
    group_whole = lax.dynamic_update_slice(group_whole, group_pair[None, None], (group_index, core, 0, 0))
    group_rows = group_whole.reshape(groups, 4, devices, VD // devices).transpose(2, 0, 1, 3)
    pieces = [
        item.reshape(devices, -1)
        for item in (
            gain_one_part,
            bias_one_part,
            gain_two_part,
            bias_two_part,
            down_bias_part,
            up_bias_whole,
            group_rows,
        )
    ]
    sums = small_sum(jnp.concatenate(pieces, axis=1))
    sums = sums[0]
    first_back = jax.vjp(lambda v: layer_norm(v, gain_one, bias_one), inputs)[1]
    tokens_grad = (grad_hidden + first_back(after(grad_normed, sums))[0]).astype(BF16)
    taken, start = [], 0
    for item in pieces:
        taken.append(sums[start : start + item.shape[1]])
        start += item.shape[1]
    first_gain_grad, first_bias_grad, second_gain_grad, second_bias_grad = taken[:4]
    down_bias_grad, up_bias_grad = taken[4:6]
    group_own = pick(taken[6].reshape(groups, 2, 2, VD // devices), group_index)
    group_gain_grad, group_bias_grad = group_own[:, 0].T, group_own[:, 1].T
    return (
        mixed,
        tokens_grad,
        first_gain_grad,
        first_bias_grad,
        query_grad,
        key_grad,
        value_grad,
        gate_grad,
        group_gain_grad,
        group_bias_grad,
        out_grad,
        second_gain_grad,
        second_bias_grad,
        up_grad,
        up_bias_grad,
        down_grad,
        down_bias_grad,
    )


def solution(mesh):
    placed = (
        P(("seq", "grp"), None),
        P("seq"),
        P("seq"),
        P("seq", "grp"),
        P("seq", "grp"),
        P("seq", "grp"),
        P("seq", "grp"),
        P("seq", "grp"),
        P("seq", "grp"),
        P("seq", None),
        P("seq"),
        P("seq"),
        P("seq", None),
        P("seq"),
        P("seq", None),
        P("seq"),
        P(("seq", "grp"), None),
        P(),
        P("grp"),
    )
    return jax.shard_map(
        body,
        mesh=mesh,
        in_specs=placed,
        out_specs=(
            P(("seq", "grp"), None),
            P(("seq", "grp"), None),
            P("seq"),
            P("seq"),
            P("seq", "grp"),
            P("seq", "grp"),
            P("seq", "grp"),
            P("seq", "grp"),
            P("seq", "grp"),
            P("seq", "grp"),
            P("seq", None),
            P("seq"),
            P("seq"),
            P("seq", None),
            P("seq"),
            P("seq", None),
            P("seq"),
        ),
        check_vma=False,
    )
```

```python
import jax
import jax.numpy as jnp
from jax import lax
from jax.experimental import pallas as pl
from jax.experimental.pallas import tpu as pltpu
from jax.sharding import PartitionSpec as P

KD = 256
VD = 512
TILE = 256
VMEM_LIMIT = 48 * 2**20
EPSILON = 1e-05

F32 = jnp.float32
BF16 = jnp.bfloat16


def dot(a, b, dims=((1,), (0,))):
    return lax.dot_general(a, b, (dims, ((), ())), preferred_element_type=F32)


def flip(block, bit):
    devices = lax.axis_size("seq")
    return lax.ppermute(block, "seq", [(i, i ^ bit) for i in range(devices)])


def hop(block, by):
    devices = lax.axis_size("seq")
    return lax.ppermute(block, "seq", [(i, i + by) for i in range(devices) if 0 <= i + by < devices])


def turn(block, by):
    groups = lax.axis_size("grp")
    return lax.ppermute(block, "grp", [(i, (i + by) % groups) for i in range(groups)])


def pick(array, index, axis=0):
    return lax.dynamic_index_in_dim(array, index, axis, keepdims=False)


def cut(array, index, size, axis):
    return lax.dynamic_slice_in_dim(array, index * size, size, axis)


def put(array, block, index, axis):
    return lax.dynamic_update_slice_in_dim(array, block, index * block.shape[axis], axis)


def after(block, *others):
    return lax.optimization_barrier((block, *others))[0]


class Stages:
    def __init__(self):
        self.last = ()

    def run(self, *sends, late=(), chain=None, joined=True):
        first = tuple(self.last if chain is None else chain) + tuple(late)
        blocks = lax.optimization_barrier(tuple(b for b, _ in sends) + first)
        came = tuple(move(block) for block, (_, move) in zip(blocks, sends))
        came = lax.optimization_barrier(came) if joined and len(came) > 1 else came
        self.last = came
        return came


def by_core(block):
    return flip(block, 1)


def by_x(block):
    return flip(block, 2)


def by_y(block):
    return flip(block, 4)


def choose(index, options):
    result = options[0]
    for i, option in enumerate(options[1:], 1):
        result = jnp.where(index == i, option, result)
    return result


def by_difference(blocks, index):
    count = len(blocks)
    return [choose(index ^ i, [blocks[d] for d in range(count)]) for i in range(count)]


class GroupLine:
    def __init__(self, group_index, count):
        self.groups = lax.axis_size("grp")
        self.index, self.count = group_index, count
        self.pieces = {}
        self.came = {"up": [], "down": []}

    def add(self, *pieces):
        for piece in lax.optimization_barrier(pieces):
            self.pieces[len(self.pieces)] = (piece, piece)

    def add_blocks(self, blocks):
        blocks = lax.optimization_barrier(tuple(blocks))
        for i in range(self.groups - 1):
            self.pieces[self.count + i] = (blocks[self.groups - 1 - i], blocks[i])

    def step(self, *late):
        step, groups = len(self.came["up"]), self.groups
        sends = []
        for way, place in (("up", self.index), ("down", groups - 1 - self.index)):
            side = 0 if way == "up" else 1
            pairs, options = [], []
            for p in range(groups - 1):
                item = step - p
                ahead = item - self.count
                live = item in self.pieces and (ahead < 0 or p + 1 <= groups - 1 - ahead)
                if live:
                    pairs.append((p, p + 1) if side == 0 else (groups - 1 - p, groups - 2 - p))
                options.append(self.pieces[item][side] if live else None)
            known = next(option for option in options if option is not None)
            sent = choose(place, [known if option is None else option for option in options])
            if step:
                sent = (sent.astype(F32) + self.came[way][-1].astype(F32)).astype(BF16)
            sends.append((sent, pairs))
        blocks = lax.optimization_barrier(tuple(sent for sent, _ in sends) + late)
        for way, block, (_, pairs) in zip(("up", "down"), blocks, sends):
            self.came[way].append(lax.ppermute(block, "grp", pairs))

    def total(self, item):
        groups = self.groups
        piece = self.pieces[item][0]
        zero = jnp.zeros_like(piece)
        below = choose(self.index, [zero] + self.came["up"][item : item + groups - 1])
        above = choose(groups - 1 - self.index, [zero] + self.came["down"][item : item + groups - 1])
        return piece.astype(F32) + below.astype(F32) + above.astype(F32)

    def last(self):
        step = self.count + self.groups - 2
        return self.came["up"][step].astype(F32) + self.came["down"][step].astype(F32)


def small_sum(block):
    bit = lax.axis_size("seq") // 2
    while bit:
        mine = lax.axis_index("seq") // bit % 2
        block = cut(block, mine, bit, 0) + flip(cut(block, 1 - mine, bit, 0), bit)
        bit //= 2
    groups, bit = lax.axis_size("grp"), 1
    while bit < groups:
        block = block + lax.ppermute(block, "grp", [(i, i ^ bit) for i in range(groups)])
        bit *= 2
    return block


def layer_norm(values, gain, bias):
    center = values - jnp.mean(values, axis=-1, keepdims=True)
    spread = jnp.mean(center * center, axis=-1, keepdims=True)
    return center * lax.rsqrt(spread + EPSILON) * gain + bias


def document_table(doc_lengths, positions):
    ends = jnp.cumsum(doc_lengths, dtype=jnp.int32)
    after = (positions[:, None] >= ends[None, :]).astype(jnp.int32)
    documents = jnp.sum(after, axis=1, dtype=jnp.int32)
    starts = jnp.sum(after * doc_lengths[None, :], axis=1, dtype=jnp.int32)
    return (documents, positions - starts)


def rotary_table(places, width):
    half = width // 2
    freqs = 10000.0 ** (-jnp.arange(half, dtype=F32) / (half - 1))
    angles = places.astype(F32)[:, None] * freqs[None, :]
    return jnp.cos(angles), jnp.sin(angles)


def rotate(values, cosine, sine):
    half = values.shape[-1] // 2
    low, high = values[:, :half], values[:, half:]
    return jnp.concatenate([low * cosine - high * sine, high * cosine + low * sine], axis=1)


def rotate_back(grads, cosine, sine):
    return rotate(grads, cosine, -sine)


def tile_bounds(starts_ref, window, first, rows, axis):
    shape = (rows, 1) if axis == 0 else (1, rows)
    position = first + lax.broadcasted_iota(jnp.int32, shape, axis)
    earliest = jnp.maximum(position - window + 1, 0)
    for d in range(starts_ref.shape[0]):
        begin = starts_ref[d]
        earliest = jnp.where(position >= begin, jnp.maximum(earliest, begin), earliest)
    return position, earliest


def retention_kernel(
    place_ref,
    starts_ref,
    decay_ref,
    query_ref,
    key_low_ref,
    key_high_ref,
    value_low_ref,
    value_high_ref,
    gate_ref,
    gain_ref,
    bias_ref,
    out_ref,
    hat_ref,
    scale_ref,
):
    half = key_low_ref.shape[0]
    log_decay = decay_ref[0]
    for tile in range(query_ref.shape[0] // TILE):
        begin = tile * TILE
        first = place_ref[0] + begin
        rows = slice(begin, begin + TILE)
        position, earliest = tile_bounds(starts_ref, place_ref[1], first, TILE, 0)
        row_decay = jnp.exp((position - first).astype(F32) * log_decay)
        total = jnp.zeros((TILE, VD), F32)
        for keys, values, low, high, offset in (
            (key_low_ref, value_low_ref, begin, half, begin - half),
            (key_high_ref, value_high_ref, 0, begin + TILE, begin * 0),
        ):
            count = high - low
            ahead = (low - begin) - (half if keys is key_low_ref else 0)
            column = first + ahead + lax.broadcasted_iota(jnp.int32, (1, count), 1)
            column_decay = jnp.exp((first - column).astype(F32) * log_decay)
            scores = dot(query_ref[rows, :], keys[low:high, :], ((1,), (1,)))
            inside = (column <= position) & (column >= earliest)
            weights = jnp.where(inside, scores * (row_decay * column_decay), 0.0).astype(BF16)
            total = total + dot(weights, values[low:high, :])
        center = total - jnp.mean(total, axis=1, keepdims=True)
        scale = lax.rsqrt(jnp.mean(center * center, axis=1, keepdims=True) + EPSILON)
        hat = center * scale
        gate = gate_ref[rows, :].astype(F32)
        silu = gate / (1.0 + jnp.exp(-gate))
        out_ref[rows, :] = (silu * (hat * gain_ref[...] + bias_ref[...])).astype(BF16)
        hat_ref[rows, :] = hat.astype(BF16)
        scale_ref[rows, :] = jnp.broadcast_to(scale, (TILE, 128))


def retention_back_kernel(
    place_ref,
    starts_ref,
    decay_ref,
    query_ref,
    key_low_ref,
    key_high_ref,
    value_low_ref,
    value_high_ref,
    gate_ref,
    gain_ref,
    bias_ref,
    hat_ref,
    scale_ref,
    grad_ref,
    query_grad_ref,
    gate_grad_ref,
    low_grad_ref,
    high_grad_ref,
    gain_grad_ref,
    bias_grad_ref,
):
    half = key_low_ref.shape[0]
    log_decay = decay_ref[0]
    gain, bias = gain_ref[...], bias_ref[...]
    gain_grad = jnp.zeros((1, VD), F32)
    bias_grad = jnp.zeros((1, VD), F32)
    low_grad_ref[...] = jnp.zeros_like(low_grad_ref)
    high_grad_ref[...] = jnp.zeros_like(high_grad_ref)
    for tile in range(query_ref.shape[0] // TILE):
        begin = tile * TILE
        first = place_ref[0] + begin
        rows = slice(begin, begin + TILE)
        hat = hat_ref[rows, :].astype(F32)
        grad = grad_ref[rows, :].astype(F32)
        gate = gate_ref[rows, :].astype(F32)
        sigmoid = 1.0 / (1.0 + jnp.exp(-gate))
        silu = gate * sigmoid
        grouped_grad = grad * silu
        gate_grad = grad * (hat * gain + bias) * (sigmoid + silu * (1.0 - sigmoid))
        gate_grad_ref[rows, :] = gate_grad.astype(BF16)
        gain_grad = gain_grad + jnp.sum(grouped_grad * hat, axis=0, keepdims=True)
        bias_grad = bias_grad + jnp.sum(grouped_grad, axis=0, keepdims=True)
        inner = grouped_grad * gain
        mean = jnp.mean(inner, axis=1, keepdims=True)
        along = jnp.mean(inner * hat, axis=1, keepdims=True)
        kept_grad = ((inner - mean - hat * along) * scale_ref[rows, :1]).astype(BF16)
        query = query_ref[rows, :]
        position, earliest = tile_bounds(starts_ref, place_ref[1], first, TILE, 1)
        row_decay = jnp.exp((position - first).astype(F32) * log_decay)
        query_grad = jnp.zeros((TILE, KD), F32)
        for keys, values, sums, low, high in (
            (key_low_ref, value_low_ref, low_grad_ref, begin, half),
            (key_high_ref, value_high_ref, high_grad_ref, 0, begin + TILE),
        ):
            count = high - low
            ahead = (low - begin) - (half if keys is key_low_ref else 0)
            column = first + ahead + lax.broadcasted_iota(jnp.int32, (count, 1), 0)
            column_decay = jnp.exp((first - column).astype(F32) * log_decay)
            inside = (column <= position) & (column >= earliest)
            mask = jnp.where(inside, row_decay * column_decay, 0.0)
            key, value = keys[low:high, :], values[low:high, :]
            weights = (dot(key, query, ((1,), (1,))) * mask).astype(BF16)
            scores = (dot(value, kept_grad, ((1,), (1,))) * mask).astype(BF16)
            sums[low:high, KD:] += dot(weights, kept_grad)
            sums[low:high, :KD] += dot(scores, query)
            query_grad = query_grad + dot(scores, key, ((0,), (0,)))
        query_grad_ref[rows, :] = query_grad
    gain_grad_ref[...] = gain_grad
    bias_grad_ref[...] = bias_grad


def whole_spec(*shape):
    return pl.BlockSpec(shape, lambda _: (0,) * len(shape))


def retention_specs(rows, low, high):
    def part(width, index):
        return pl.BlockSpec((rows, width), lambda _: (index, 0))

    smem = pl.BlockSpec(memory_space=pltpu.SMEM)
    return [smem] * 3 + [
        part(KD, high[1]),
        part(KD, low),
        part(KD, high[0]),
        part(VD, low),
        part(VD, high[0]),
        part(VD, high[1]),
        whole_spec(1, VD),
        whole_spec(1, VD),
    ]


def retention(place, starts, decay, queries, keys, values, gate, gain, bias, rows, low, high):
    cost = pl.CostEstimate(flops=rows * 1966080, bytes_accessed=rows * 8192, transcendentals=0)
    return pl.pallas_call(
        retention_kernel,
        out_shape=(
            jax.ShapeDtypeStruct((rows, VD), BF16),
            jax.ShapeDtypeStruct((rows, VD), BF16),
            jax.ShapeDtypeStruct((rows, 128), F32),
        ),
        grid=(1,),
        in_specs=retention_specs(rows, low, high),
        out_specs=(whole_spec(rows, VD), whole_spec(rows, VD), whole_spec(rows, 128)),
        compiler_params=pltpu.CompilerParams(vmem_limit_bytes=VMEM_LIMIT),
        cost_estimate=cost,
    )(place, starts, decay, queries, keys[0], keys[1], values[0], values[1], gate, gain, bias)


def retention_back(
    place, starts, decay, queries, keys, values, gate, gain, bias, hat, scale, grad, rows, low, high
):
    cost = pl.CostEstimate(flops=rows * 4587520, bytes_accessed=rows * 16384, transcendentals=0)
    part = pl.BlockSpec((rows, VD), lambda _: (high[1], 0))
    return pl.pallas_call(
        retention_back_kernel,
        out_shape=(
            jax.ShapeDtypeStruct((rows, KD), F32),
            jax.ShapeDtypeStruct((rows, VD), BF16),
            jax.ShapeDtypeStruct((rows, KD + VD), F32),
            jax.ShapeDtypeStruct((rows, KD + VD), F32),
            jax.ShapeDtypeStruct((1, VD), F32),
            jax.ShapeDtypeStruct((1, VD), F32),
        ),
        grid=(1,),
        in_specs=retention_specs(rows, low, high)
        + [whole_spec(rows, VD), whole_spec(rows, 128), part],
        out_specs=(
            whole_spec(rows, KD),
            whole_spec(rows, VD),
            whole_spec(rows, KD + VD),
            whole_spec(rows, KD + VD),
            whole_spec(1, VD),
            whole_spec(1, VD),
        ),
        compiler_params=pltpu.CompilerParams(vmem_limit_bytes=VMEM_LIMIT),
        cost_estimate=cost,
    )(place, starts, decay, queries, keys[0], keys[1], values[0], values[1], gate, gain, bias, hat, scale, grad)


def feed_kernel(
    normed_ref,
    cotangent_ref,
    up_ref,
    down_ref,
    bias_ref,
    activated_ref,
    grad_pre_ref,
    mixed_ref,
    grad_ref,
    bias_grad_ref,
):
    up, down = up_ref[...], down_ref[...]
    pre = dot(normed_ref[...], up) + bias_ref[...]
    grad_act = dot(cotangent_ref[...], down, ((1,), (1,)))
    share = 0.5 + 0.5 * lax.erf(pre * 0.7071067811865476)
    bell = jnp.exp(-0.5 * pre * pre) * 0.3989422804014327
    activated = (pre * share).astype(BF16)
    grad_pre = (grad_act * (share + pre * bell)).astype(BF16)
    activated_ref[...] = activated
    grad_pre_ref[...] = grad_pre
    mixed_ref[...] = dot(activated, down).astype(BF16)
    grad_ref[...] = dot(grad_pre, up, ((1,), (1,))).astype(BF16)

    @pl.when(pl.program_id(0) == 0)
    def _():
        bias_grad_ref[...] = jnp.zeros_like(bias_grad_ref)

    bias_grad_ref[...] += jnp.sum(grad_pre.astype(F32), axis=0, keepdims=True)


def feed(normed, cotangent, up, down, bias):
    rows, width = normed.shape
    hidden = up.shape[1]

    def tiled(columns):
        return pl.BlockSpec((TILE, columns), lambda i: (i, 0))

    cost = pl.CostEstimate(
        flops=rows * width * hidden * 8, bytes_accessed=rows * width * 8, transcendentals=0
    )
    return pl.pallas_call(
        feed_kernel,
        out_shape=(
            jax.ShapeDtypeStruct((rows, hidden), BF16),
            jax.ShapeDtypeStruct((rows, hidden), BF16),
            jax.ShapeDtypeStruct((rows, width), BF16),
            jax.ShapeDtypeStruct((rows, width), BF16),
            jax.ShapeDtypeStruct((1, hidden), F32),
        ),
        grid=(rows // TILE,),
        in_specs=[
            tiled(width),
            tiled(width),
            whole_spec(*up.shape),
            whole_spec(*down.shape),
            whole_spec(1, hidden),
        ],
        out_specs=(tiled(hidden), tiled(hidden), tiled(width), tiled(width), whole_spec(1, hidden)),
        compiler_params=pltpu.CompilerParams(vmem_limit_bytes=VMEM_LIMIT),
        cost_estimate=cost,
    )(normed, cotangent, up, down, bias)
def body(
    tokens,
    first_gain,
    first_bias,
    query_weight,
    key_weight,
    value_weight,
    gate_weight,
    group_gain,
    group_bias,
    out_weight,
    second_gain,
    second_bias,
    up_weight,
    up_bias,
    down_weight,
    down_bias,
    cotangent,
    doc_lengths,
    windows,
):
    devices, groups = lax.axis_size("seq"), lax.axis_size("grp")
    seq_index, group_index = lax.axis_index("seq"), lax.axis_index("grp")
    chips, quads = devices // 2, devices // 4
    core, chip = seq_index % 2, seq_index // 2
    quarter, quad = seq_index % 4, seq_index // 4
    own_rows, width = tokens.shape
    part = width // devices
    rows = own_rows * groups
    pair_rows = 2 * rows
    ff = up_weight.shape[1]
    ff_part, ff_quarter = ff // devices, ff // 4
    small_mesh = devices == 8
    stages = Stages()

    def head_columns(j):
        return jnp.concatenate(
            [
                cut(query_weight, j, KD, 1),
                cut(key_weight, j, KD, 1),
                cut(value_weight, j, VD, 1),
                cut(gate_weight, j, VD, 1),
            ],
            axis=1,
        )

    mine = head_columns(core)
    theirs = by_core(head_columns(1 - core))
    low_rows = jnp.where(core == 0, mine, theirs)
    high_rows = jnp.where(core == 0, theirs, mine)
    columns = mine.shape[1]

    small = [first_gain, first_bias, second_gain, second_bias, down_bias, up_bias]
    small += [group_gain.T.reshape(-1), group_bias.T.reshape(-1)]
    sizes = [item.shape[0] for item in small]
    packed = lax.all_gather(after(jnp.concatenate(small)[None], low_rows, high_rows), "seq", axis=0, tiled=True).astype(F32)
    whole, start = [], 0
    for size in sizes:
        whole.append(packed[:, start : start + size])
        start += size
    gain_one, bias_one, gain_two, bias_two, down_bias_full, up_bias_full = (
        item.reshape(-1) for item in whole[:6]
    )
    group_gain_f, group_bias_f = (
        pick(item.reshape(devices, 2, -1), core, 1).reshape(1, VD) for item in whole[6:]
    )
    up_bias_quarter = pick(up_bias_full.reshape(quads, 4, ff_part), quarter, 1).reshape(1, ff_quarter)

    inputs = tokens.astype(F32)
    normed = layer_norm(inputs, gain_one, bias_one).astype(BF16)
    gathered = lax.all_gather(normed, "grp", axis=0, tiled=True)

    base = chip * pair_rows
    positions = base + jnp.arange(pair_rows, dtype=jnp.int32)
    places = document_table(doc_lengths, positions)[1]
    doc_starts = jnp.cumsum(doc_lengths, dtype=jnp.int32) - doc_lengths
    cosine, sine = rotary_table(places, KD)
    def join_chips(low, high):
        held = {0: jnp.stack([low, high])}
        for bit in range(1, devices.bit_length() - 1):
            held.update({d | (1 << (bit - 1)): flip(v, 1 << bit) for d, v in list(held.items())})
        return {d: (v[0], v[1]) for d, v in held.items()}

    def quarter_columns(q):
        return [
            lax.dynamic_slice_in_dim(up_weight, (q + 4 * m) * ff_part, ff_part, 1) for m in range(quads)
        ]

    up_sent = jnp.concatenate(quarter_columns(quarter ^ 2) + quarter_columns(quarter ^ 3), axis=1)
    if small_mesh:
        half_low = VD // 2
        out_low, out_high = out_weight[:half_low], out_weight[half_low:]
        low_x, high_y = stages.run((low_rows, by_x), (high_rows, by_y))
        high_xy, low_xy = stages.run(
            (jnp.stack([high_rows, high_y]), by_x), (jnp.stack([low_rows, low_x]), by_y)
        )
        head_held = {
            0: (low_rows, high_rows),
            1: (low_x, high_xy[0]),
            2: (low_xy[0], high_y),
            3: (low_xy[1], high_xy[1]),
        }
        two_x, down_y = stages.run((jnp.stack([up_sent, cotangent]), by_x), (down_weight, by_y))
        up_x, cotangent_x = two_x[0], two_x[1]
        gathered = after(gathered, high_xy, low_xy, cosine, sine)
    else:
        head_held = join_chips(low_rows, high_rows)
        up_x = by_x(up_sent)
    head_weight = jnp.zeros((chips, 2, part, columns), BF16)
    for d, (low, high) in head_held.items():
        head_weight = put(head_weight, jnp.stack([low, high])[None], chip ^ d, 0)
    head_weight = head_weight.reshape(width, columns)

    up_core = by_core(
        jnp.stack([jnp.concatenate(quarter_columns(quarter ^ 1), axis=1), up_x[:, ff_quarter:]])
    )
    up_own = jnp.concatenate(quarter_columns(quarter), axis=1)
    up_four = jnp.stack([up_own, up_core[0], up_x[:, :ff_quarter], up_core[1]])

    beside = by_core(gathered)
    pair_normed = jnp.concatenate(
        [jnp.where(core == 0, gathered, beside), jnp.where(core == 0, beside, gathered)], axis=0
    )

    key_scale = KD ** (-0.5)
    key_pre = dot(pair_normed, head_weight[:, KD : 2 * KD])
    keys = (rotate(key_pre, cosine, sine) * key_scale).astype(BF16)
    values = dot(pair_normed, head_weight[:, 2 * KD : 2 * KD + VD]).astype(BF16)
    halo = jnp.concatenate([keys[rows:], values[rows:]], axis=1)
    if small_mesh:
        weights_last = stages.last
        (halo,) = stages.run((halo, lambda v: hop(v, 2)), chain=(high_xy, low_xy))
    else:
        halo = hop(halo, 2)
    query_pre = dot(pair_normed, head_weight[:, :KD])
    gate_pre = dot(pair_normed, head_weight[:, 2 * KD + VD :]).astype(BF16)
    queries = rotate(query_pre, cosine, sine).astype(BF16)
    halo = (halo[:, :KD], halo[:, KD:])
    head_index = (group_index * 2 + core).astype(F32)
    log_decay = jnp.log1p(-jnp.exp2(-5.0 - head_index)).reshape(1)
    window = windows[0]

    shared = (doc_starts, log_decay, queries)
    late_rows, early_rows = (0, (1, 1)), (0, (0, 0))
    late_place = jnp.stack([base + rows, window])
    early_place = jnp.stack([base, window])
    late_keys, late_values = (keys, keys), (values, values)
    early_keys, early_values = (halo[0], keys), (halo[1], values)
    gated = (gate_pre, group_gain_f, group_bias_f)
    late_out, late_hat, late_scale = retention(
        late_place, *shared, late_keys, late_values, *gated, rows, *late_rows
    )
    early_out, early_hat, early_scale = retention(
        early_place, *shared, early_keys, early_values, *gated, rows, *early_rows
    )

    if small_mesh:
        out_low_x, out_high_y = stages.run(
            (out_low, by_x), (out_high, by_y), chain=weights_last, late=(gate_pre,)
        )
        out_high_xy, out_low_xy, up_y = stages.run(
            (jnp.stack([out_high, out_high_y]), by_x),
            (jnp.stack([out_low, out_low_x]), by_y),
            (up_four, by_y),
            chain=(),
            joined=False,
        )
        out_held = {
            0: (out_low, out_high),
            1: (out_low_x, out_high_xy[0]),
            2: (out_low_xy[0], out_high_y),
            3: (out_low_xy[1], out_high_xy[1]),
        }
        out_head = jnp.zeros((chips, 2, half_low, width), BF16)
        for d, (low, high) in out_held.items():
            out_head = put(out_head, jnp.stack([low, high])[None], chip ^ d, 0)
        out_head = out_head.reshape(groups * VD, width)
    else:
        out_head = lax.all_gather(out_weight, "seq", axis=0, tiled=True)
        out_head = pick(out_head.reshape(groups, 2, VD, width), core, 1).reshape(groups * VD, width)
    up_held, down_held = {0: up_four}, {0: down_weight}
    if small_mesh:
        up_held[1] = up_y
        down_held[1] = down_y
    else:
        for bit in range(2, devices.bit_length() - 1):
            for held in (up_held, down_held):
                held.update({d | (1 << (bit - 2)): flip(v, 1 << bit) for d, v in list(held.items())})
    up_quarter = jnp.zeros((devices, part, ff_quarter), BF16)
    for e, four in up_held.items():
        for d in range(4):
            up_quarter = put(up_quarter, four[d : d + 1], seq_index ^ (4 * e + d), 0)
    up_quarter = up_quarter.reshape(width, ff_quarter)
    down_quarter = jnp.concatenate(by_difference(down_held, quad), axis=0)

    def with_core(two):
        return jnp.concatenate([two, by_core(two)], axis=0)

    if not small_mesh:
        cotangent_x = by_x(cotangent)
    near_cotangent, far_cotangent = with_core(cotangent), with_core(cotangent_x)

    def exchange(blocks):
        return lax.all_to_all(blocks, "grp", split_axis=0, concat_axis=0, tiled=True)

    def to_tokens(early, late):
        parted = [item.reshape(groups, own_rows, VD) for item in (early, late)]
        came = exchange(jnp.concatenate(parted, axis=1))
        return jnp.concatenate(list(came), axis=1)

    def to_heads(block):
        sent = jnp.stack([block[:, i * VD : (i + 1) * VD] for i in range(groups)])
        came = exchange(sent).reshape(groups, 2, own_rows, VD)
        return jnp.concatenate([came[:, 0].reshape(rows, VD), came[:, 1].reshape(rows, VD)])

    def pair_sum(block, size, kind):
        mine = cut(block, core, size, 0)
        return mine + by_core(cut(block, 1 - core, size, 0).astype(kind)).astype(F32)

    def pair_rows_of(block):
        beside = by_core(block)
        return jnp.concatenate(
            [jnp.where(core == 0, block, beside), jnp.where(core == 0, beside, block)], axis=0
        )

    by_token = to_tokens(early_out, late_out)
    hidden = inputs + pair_sum(dot(by_token, out_head), own_rows, F32)
    normed_two = layer_norm(hidden, gain_two, bias_two).astype(BF16)
    normed_x = by_x(normed_two)
    near_normed, far_normed = with_core(normed_two), with_core(normed_x)
    weights = (up_quarter, down_quarter, up_bias_quarter)
    near_activated, near_grad_pre, near_mixed, near_grad, near_bias = feed(near_normed, near_cotangent, *weights)
    far_activated, far_grad_pre, far_mixed, far_grad, far_bias = feed(far_normed, far_cotangent, *weights)
    up_bias_part = near_bias + far_bias
    grad_out = cotangent.astype(F32)
    down_bias_part = jnp.sum(grad_out, axis=0)

    def plus(mine, came):
        return mine.astype(F32) + came.astype(F32)

    def pair_part(block):
        return plus(block[:own_rows], by_core(block[own_rows:]))

    far_grad = pair_part(far_grad).astype(BF16)
    activated = jnp.concatenate([near_activated, far_activated])
    quad_cotangent = jnp.concatenate([near_cotangent, far_cotangent])
    down_part = dot(activated, quad_cotangent, ((0,), (0,))).astype(BF16).reshape(quads, ff_part, width)
    if small_mesh:
        grad_x, down_y = stages.run((far_grad, by_x), (pick(down_part, 1 - quad), by_y), chain=(), joined=False)
    else:
        grad_x = by_x(far_grad)
    grad_normed_two = plus(pair_part(near_grad), grad_x)
    second_back = jax.vjp(layer_norm, hidden, gain_two, bias_two)[1]
    hidden_part, gain_two_part, bias_two_part = second_back(grad_normed_two)
    grad_hidden = grad_out + hidden_part
    grad_attend = pair_rows_of(grad_hidden.astype(BF16))
    grad_by_token = dot(grad_attend, out_head, ((1,), (1,))).astype(BF16)
    grad_heads = to_heads(grad_by_token)

    quad_normed = jnp.concatenate([near_normed, far_normed])
    quad_grad_pre = jnp.concatenate([near_grad_pre, far_grad_pre])
    up_part = dot(quad_normed, quad_grad_pre, ((0,), (0,))).astype(BF16).reshape(quads, 4, part, ff_quarter)
    out_part = dot(by_token, grad_attend, ((0,), (0,))).astype(BF16)

    def split_chips(parts):
        held, bit = dict(parts), 1
        while bit < chips:
            sent = {d: flip(v.astype(BF16), 2 * bit) for d, v in held.items() if d & bit}
            held = {
                d: v.astype(F32) + sent[d | bit].astype(F32) for d, v in held.items() if not d & bit
            }
            bit *= 2
        return held[0]

    def split_quads(block):
        held, bit = {d: pick(block, quad ^ d) for d in range(quads)}, 1
        while bit < quads:
            sent = {d: flip(v.astype(BF16), 4 * bit) for d, v in held.items() if d & bit}
            held = {
                d: v.astype(F32) + sent[d | bit].astype(F32) for d, v in held.items() if not d & bit
            }
            bit *= 2
        return held[0]

    def up_to_owners(up_four, up_x):
        up_core = by_core(jnp.stack([pick(up_four, quarter ^ 1), up_x[1]]))
        up_blocks = by_difference([pick(up_four, quarter), up_core[0], up_x[0], up_core[1]], quarter)
        return jnp.concatenate(
            [block[:, m * ff_part : (m + 1) * ff_part] for m in range(quads) for block in up_blocks], axis=1
        )

    def up_x_sent(up_four):
        return jnp.stack([pick(up_four, quarter ^ 2), pick(up_four, quarter ^ 3)])

    mixed_sent = pair_part(far_mixed).astype(BF16)
    if small_mesh:
        down_sum = plus(pick(down_part, quad), down_y).astype(BF16)
        out_part = out_part.reshape(chips, 2, half_low, width)
        low, high = ([pick(out_part[:, i], chip ^ d) for d in range(chips)] for i in (0, 1))
        high_x, low_y = stages.run(
            (jnp.stack([high[1], high[3]]), by_x),
            (jnp.stack([low[2], low[3]]), by_y),
            chain=(grad_by_token,),
        )
        low_x, high_y = stages.run(
            (plus(low[1], low_y[1]).astype(BF16), by_x),
            (plus(high[2], high_x[1]).astype(BF16), by_y),
            late=(grad_heads,),
        )
        low_sum = plus(plus(low[0], low_y[0]), low_x).astype(BF16)
        high_sum = plus(plus(high[0], high_x[0]), high_y).astype(BF16)
    else:
        mixed_x = by_x(mixed_sent)
        down_sum = split_quads(down_part).astype(BF16)
        up_four = split_quads(up_part).astype(BF16)
        spread = jnp.zeros((groups, 2, VD, width), BF16)
        spread = put(spread, out_part.reshape(groups, 1, VD, width), core, 1)
        out_sum = lax.psum_scatter(
            spread.reshape(groups * 2 * VD, width), "seq", scatter_dimension=0, tiled=True
        )
        low_sum, high_sum = jnp.split(out_sum, 2)
    half = down_sum.shape[0] // 2
    line = GroupLine(group_index, 6)
    line.add(down_sum[:half], down_sum[half:])
    line.add(low_sum, high_sum)

    early_query, early_gate, later, early_own, early_gain, early_bias = retention_back(
        early_place, *shared, early_keys, early_values, *gated, early_hat, early_scale, grad_heads, rows, *early_rows
    )
    late_query, late_gate, late_own, late_end, late_gain, late_bias = retention_back(
        late_place, *shared, late_keys, late_values, *gated, late_hat, late_scale, grad_heads, rows, *late_rows
    )
    line.step(grad_heads)
    line.step(late_gate)
    group_gain_part, group_bias_part = early_gain + late_gain, early_bias + late_bias
    later = later.astype(BF16)
    if small_mesh:
        out_last = stages.last
        (later,) = stages.run((later, lambda v: hop(v, -2)), chain=(high_x, low_y))
        mixed_x, up_y = stages.run(
            (mixed_sent, by_x), (pick(up_part, 1 - quad), by_y), chain=out_last, late=(late_gate,)
        )
        up_four = plus(pick(up_part, quad), up_y).astype(BF16)
    else:
        later = hop(later, -2)
    chunk_shape = low_sum.shape
    line.add(*(item.reshape(chunk_shape) for item in jnp.split(up_four.reshape(-1), 2)))

    def projection_grads(query, own, gate, begin):
        near = slice(begin, begin + rows)
        turned = (cosine[near], sine[near])
        return jnp.concatenate(
            [
                rotate_back(query, *turned).astype(BF16),
                (rotate_back(own[:, :KD], *turned) * key_scale).astype(BF16),
                own[:, KD:].astype(BF16),
                gate,
            ],
            axis=1,
        )

    early_grads = projection_grads(early_query, early_own + late_own, early_gate, 0)
    line.step(early_grads)
    late_grads = projection_grads(late_query, late_end + later.astype(F32), late_gate, rows)
    line.step(late_grads)
    grads = jnp.concatenate([early_grads, late_grads])

    theirs_part = dot(cut(grads, 1 - core, rows, 0), head_weight, ((1,), (1,))).astype(BF16)
    normed_part = dot(cut(grads, core, rows, 0), head_weight, ((1,), (1,))) + by_core(theirs_part).astype(F32)
    blocks = normed_part.astype(BF16).reshape(groups, own_rows, width)
    own_block = pick(normed_part.reshape(groups, own_rows, width), group_index)
    if small_mesh:
        line.add_blocks(blocks)
        for _ in range(5):
            line.step()
        from_groups = line.last()
    else:
        for _ in range(4):
            line.step()
        block_line = GroupLine(group_index, 0)
        block_line.add_blocks(blocks)
        for _ in range(groups - 1):
            block_line.step()
        from_groups = block_line.last()
    grad_normed = own_block + from_groups
    down_grad = jnp.concatenate([line.total(0), line.total(1)])
    out_grad = jnp.concatenate([line.total(2), line.total(3)])
    up_four = jnp.concatenate([line.total(4).reshape(-1), line.total(5).reshape(-1)]).astype(BF16)
    up_four = up_four.reshape(4, part, ff_quarter)
    head_part = dot(pair_normed, grads, ((0,), (0,))).astype(BF16)
    product_part = jnp.sum(head_part.astype(F32) * head_weight.astype(F32), axis=1)
    bias_one_part = jnp.sum(head_weight.astype(F32) * jnp.sum(grads.astype(F32), axis=0)[None], axis=1)
    gain_one_part = (product_part - bias_one * bias_one_part) / gain_one
    head_part = head_part.reshape(chips, 2, part, columns)
    parts = {d: pick(head_part, chip ^ d) for d in range(chips)}
    if small_mesh:
        high_x, low_y = stages.run(
            (jnp.stack([parts[1][1], parts[3][1]]), by_x),
            (jnp.stack([parts[2][0], parts[3][0]]), by_y),
            late=(normed_part,),
        )
        low_x, high_y = stages.run(
            (plus(parts[1][0], low_y[1]).astype(BF16), by_x),
            (plus(parts[2][1], high_x[1]).astype(BF16), by_y),
        )
        low_sum = plus(plus(parts[0][0], low_y[0]), low_x)
        high_sum = plus(plus(parts[0][1], high_x[0]), high_y)
    else:
        low_sum, high_sum = split_chips(parts)
    up_grad = up_to_owners(up_four, by_x(up_x_sent(up_four))).astype(F32)
    mixed = (hidden + plus(pair_part(near_mixed), mixed_x) + down_bias_full).astype(BF16)
    own_head = jnp.where(core == 0, low_sum, high_sum)
    other_head = by_core(jnp.where(core == 0, high_sum, low_sum).astype(BF16)).astype(F32)
    first_head = jnp.where(core == 0, own_head, other_head)
    second_head = jnp.where(core == 0, other_head, own_head)

    def both_heads(start, size):
        return jnp.concatenate(
            [first_head[:, start : start + size], second_head[:, start : start + size]], axis=1
        )

    query_grad, key_grad = both_heads(0, KD), both_heads(KD, KD)
    value_grad, gate_grad = both_heads(2 * KD, VD), both_heads(2 * KD + VD, VD)

    up_bias_whole = put(jnp.zeros((quads, 4, ff_part), F32), up_bias_part.reshape(quads, 1, ff_part), quarter, 1)
    group_whole = jnp.zeros((groups, 2, 2, VD), F32)
    group_pair = jnp.stack([group_gain_part.reshape(-1), group_bias_part.reshape(-1)])
    group_whole = lax.dynamic_update_slice(group_whole, group_pair[None, None], (group_index, core, 0, 0))
    group_rows = group_whole.reshape(groups, 4, devices, VD // devices).transpose(2, 0, 1, 3)
    pieces = [
        item.reshape(devices, -1)
        for item in (
            gain_one_part,
            bias_one_part,
            gain_two_part,
            bias_two_part,
            down_bias_part,
            up_bias_whole,
            group_rows,
        )
    ]
    sums = small_sum(jnp.concatenate(pieces, axis=1))
    sums = sums[0]
    first_back = jax.vjp(lambda v: layer_norm(v, gain_one, bias_one), inputs)[1]
    tokens_grad = (grad_hidden + first_back(after(grad_normed, sums))[0]).astype(BF16)
    taken, start = [], 0
    for item in pieces:
        taken.append(sums[start : start + item.shape[1]])
        start += item.shape[1]
    first_gain_grad, first_bias_grad, second_gain_grad, second_bias_grad = taken[:4]
    down_bias_grad, up_bias_grad = taken[4:6]
    group_own = pick(taken[6].reshape(groups, 2, 2, VD // devices), group_index)
    group_gain_grad, group_bias_grad = group_own[:, 0].T, group_own[:, 1].T
    return (
        mixed,
        tokens_grad,
        first_gain_grad,
        first_bias_grad,
        query_grad,
        key_grad,
        value_grad,
        gate_grad,
        group_gain_grad,
        group_bias_grad,
        out_grad,
        second_gain_grad,
        second_bias_grad,
        up_grad,
        up_bias_grad,
        down_grad,
        down_bias_grad,
    )


def solution(mesh):
    placed = (
        P(("seq", "grp"), None),
        P("seq"),
        P("seq"),
        P("seq", "grp"),
        P("seq", "grp"),
        P("seq", "grp"),
        P("seq", "grp"),
        P("seq", "grp"),
        P("seq", "grp"),
        P("seq", None),
        P("seq"),
        P("seq"),
        P("seq", None),
        P("seq"),
        P("seq", None),
        P("seq"),
        P(("seq", "grp"), None),
        P(),
        P("grp"),
    )
    return jax.shard_map(
        body,
        mesh=mesh,
        in_specs=placed,
        out_specs=(
            P(("seq", "grp"), None),
            P(("seq", "grp"), None),
            P("seq"),
            P("seq"),
            P("seq", "grp"),
            P("seq", "grp"),
            P("seq", "grp"),
            P("seq", "grp"),
            P("seq", "grp"),
            P("seq", "grp"),
            P("seq", None),
            P("seq"),
            P("seq"),
            P("seq", None),
            P("seq"),
            P("seq", None),
            P("seq"),
        ),
        check_vma=False,
    )
```
